256 devices in a mesh: rep: 8 (over x, y_lo), row: 32 (over y_hi, z, core).
Axes of the slice: x: 4, y: 4 (y_hi: 2, y_lo: 2; y = y_hi * 2 + y_lo), z: 8, core: 2. Of those that a mesh axis runs over, the one named last changes fastest.
Arguments:
- features: bfloat16 [32, 2048, 128], P('row', 'rep'), may hold values from -6 to 6
- weight: bfloat16 [128, 128], replicated, may hold values from -0.5 to 0.5
- cotangent: bfloat16 [32, 2048, 128], P('row', 'rep'), may hold values from -6 to 6
- tiles: bfloat16 [32, 8, 256, 128, 128], P('row', 'rep'), may hold values from -0.0625 to 0.0625
- row_ids: int32 [32, 8, 256], P('row', 'rep'), may hold values from 0 to 15
- col_ids: int32 [32, 8, 256], P('row', 'rep'), may hold values from 0 to 63
- counts: int32 [32, 8], P('row', 'rep'), may hold values from 64 to 256, as said below
Outputs:
- hidden: bfloat16 [32, 2048, 128], P('row', 'rep')
- grad_features: bfloat16 [32, 2048, 128], P('row', 'rep')
- grad_weight: float32 [128, 128], replicated
The draws below stay inside these ranges and needn't reach their ends.
Inputs may be any that keep to these rules, and one draw needn't show every extreme that they name: In every draw some group and slab has exactly 256 tiles in use. A count above 128 is exactly 256; for every slab r and group i < 16, counts[i, r] and counts[i + 16, r] are never both above 128.
All inputs are finite; a program needn't handle non-finite values.
Results may differ from the reference program's by a relative error of at most 0.017.
Values may be sent and summed in bfloat16 or wider, within the bound.
No kernel may reach another device: no remote copies, remote signals or barrier semaphores. Data moves between devices by JAX's collectives and lax.ppermute only.
A program may use at most 128 MiB of HBM per device.

```python
import jax
import jax.numpy as jnp
from jax import lax

F = 128
BLOCK = 128
NODES = 256
CAP = 256
GROUPS = 32
SLABS = 8
RB = 16
CB = 64


def draw_counts(key, part):
    key = jax.random.fold_in(key, 7)
    first, second, third = jax.random.split(key, 3)
    half = GROUPS // 2
    base = jax.random.randint(first, (GROUPS, SLABS), CAP // 4, CAP // 2 + 1)
    order = jax.random.permutation(second, half * SLABS).reshape(half, SLABS)
    heavy = max(1, GROUPS * SLABS // 8)
    chosen = order < heavy
    side = jax.random.randint(third, (half, SLABS), 0, 2)
    upper = chosen & (side == 0)
    lower = chosen & (side == 1)
    marks = jnp.concatenate([upper, lower], axis=0)
    filled = jnp.where(marks, CAP, base)
    return filled.astype(jnp.int32)


def touch_ends(entries, key, smallest, high):
    shape = entries.shape
    index_at = [jax.random.randint(jax.random.fold_in(key, axis), (), 0, shape[axis]) for axis in range(len(shape))]
    entries = entries.at[tuple(index_at)].set(smallest)
    longest = shape.index(max(shape))
    index_at[longest] = (index_at[longest] + 1) % shape[longest]
    return entries.at[tuple(index_at)].set(high)


def block_scale(key, shape, shards, low, largest):
    level, own = 1.0, jax.random.fold_in(key, 6)
    for dim, shards_of in shards:
        draws = jnp.exp(jax.random.uniform(jax.random.fold_in(own, dim), (shards_of,), jnp.float32, low / len(shards), largest / len(shards)))
        level = level * jnp.repeat(draws, shape[dim] // shards_of).reshape([-1 if axis == dim else 1 for axis in range(len(shape))])
    return level


def gaussian(rng, extent, deviation, bound, cuts=(), held_as=jnp.bfloat16):
    drawn = jax.random.normal(rng, extent, jnp.float32) * deviation
    if len(cuts) > 0:
        drawn = block_scale(rng, extent, cuts, -0.22, 0.18) * drawn
    return jnp.clip(drawn, min=-bound, max=bound).astype(held_as)


def setup_inputs(seed: int = 0) -> dict:
    seeds = jax.random.split(jax.random.key(seed), 8)
    return {
        "features": gaussian(seeds[0], (GROUPS, SLABS * NODES, F), 1.0, 6.0, ((0, 32), (1, 8))),
        "weight": gaussian(seeds[1], (F, F), F ** -0.5, 0.5),
        "cotangent": gaussian(seeds[2], (GROUPS, SLABS * NODES, F), 1.0, 6.0, ((0, 32), (1, 8))),
        "tiles": gaussian(seeds[3], (GROUPS, SLABS, CAP, BLOCK, BLOCK), (CAP * 64 * BLOCK // NODES) ** -0.5, 0.0625, ((0, 32), (1, 8))),
        "row_ids": touch_ends(jax.random.randint(seeds[4], (GROUPS, SLABS, CAP), 0, RB), jax.random.fold_in(seeds[4], 1), 0, RB - 1).astype(jnp.int32),
        "col_ids": touch_ends(jax.random.randint(seeds[5], (GROUPS, SLABS, CAP), 0, CB), jax.random.fold_in(seeds[5], 1), 0, CB - 1).astype(jnp.int32),
        "counts": draw_counts(jax.random.fold_in(seeds[7], 71), 0),
    }


def reference(features, weight, cotangent, tiles, row_ids, col_ids, counts):
    flat = features.reshape(-1, F)
    xw = jnp.dot(flat, weight, preferred_element_type=jnp.float32).astype(jnp.bfloat16)
    xw = xw.reshape(GROUPS, SLABS, NODES, F)
    slab_feats = jnp.transpose(xw, (1, 0, 2, 3)).reshape(SLABS, CB, BLOCK, F)

    def group_step(carry, inputs):
        tile_g, rows_g, cols_g, count_g, cot_g = inputs
        valid = (jnp.arange(CAP, dtype=jnp.int32)[None, :] < count_g[:, None]).astype(jnp.float32)
        tile_f = tile_g.astype(jnp.float32)
        picked = jax.vmap(lambda table, index: jnp.take(table, index, axis=0))(slab_feats, cols_g)
        products = jnp.einsum("rtab,rtbf->rtaf", tile_f, picked.astype(jnp.float32))
        products = products * valid[:, :, None, None]
        onehot_rows = (rows_g[:, :, None] == jnp.arange(RB, dtype=jnp.int32)[None, None, :]).astype(jnp.float32)
        zsum = jnp.einsum("rtq,rtaf->qaf", onehot_rows, products).reshape(RB * BLOCK, F)
        sigma = jax.nn.sigmoid(zsum)
        out_rows = (zsum * sigma).astype(jnp.bfloat16)
        grad_pre = (cot_g.astype(jnp.float32) * sigma * (1.0 + zsum * (1.0 - sigma))).astype(jnp.bfloat16)
        grad_blocks = grad_pre.reshape(RB, BLOCK, F)
        back_in = jnp.take(grad_blocks, rows_g, axis=0).astype(jnp.float32)
        back = jnp.einsum("rtab,rtaf->rtbf", tile_f, back_in) * valid[:, :, None, None]
        onehot_cols = (cols_g[:, :, None] == jnp.arange(CB, dtype=jnp.int32)[None, None, :]).astype(jnp.float32)
        carry = carry + jnp.einsum("rtc,rtbf->rcbf", onehot_cols, back)
        return carry, out_rows

    start = jnp.zeros((SLABS, CB, BLOCK, F), jnp.float32)
    slab_grad, hidden = lax.scan(group_step, start, (tiles, row_ids, col_ids, counts, cotangent))
    grad_sum = slab_grad.reshape(SLABS, GROUPS, NODES, F)
    grad_sum = jnp.transpose(grad_sum, (1, 0, 2, 3)).reshape(GROUPS * SLABS * NODES, F)
    grad_xw = grad_sum.astype(jnp.bfloat16)
    grad_features = jnp.dot(grad_xw, weight.T, preferred_element_type=jnp.float32).astype(jnp.bfloat16)
    grad_weight = jnp.dot(flat.T, grad_xw, preferred_element_type=jnp.float32)
    return hidden, grad_features.reshape(GROUPS, SLABS * NODES, F), grad_weight
```

```python
import jax
import jax.numpy as jnp
from jax import lax
from jax.experimental import pallas as pl
from jax.experimental.pallas import tpu as pltpu
from jax.sharding import Mesh, PartitionSpec as P

CHUNK = 32
BLOCK = 128
ROWS = 16
COLS = 64
HALF = COLS // 2
SIZES = (4, 2, 2, 8, 2)
AXES = ("x", "ylo", "yhi", "z", "core")
REP = ("x", "ylo")
COLUMN = ("yhi", "z")
ROW = ("yhi", "z", "core")
SWAP = ((0, 1), (1, 0))


def tile_copy(tiles, buffer, sems, chunk):
    span = pl.ds(chunk * CHUNK, CHUNK)
    return pltpu.make_async_copy(tiles.at[span], buffer.at[span], sems.at[chunk])


def forward_kernel(count, rows, cols, tiles, own, other, out, buffer, xs, acc, sems, xsems):
    chunks = (count[0] + CHUNK - 1) // CHUNK
    first = pltpu.make_async_copy(own, xs.at[pl.ds(0, HALF)], xsems.at[0])
    second = pltpu.make_async_copy(other, xs.at[pl.ds(HALF, HALF)], xsems.at[1])
    first.start()
    second.start()

    @pl.loop(0, chunks)
    def _(c):
        tile_copy(tiles, buffer, sems, c).start()

    acc[...] = jnp.zeros_like(acc)
    first.wait()
    second.wait()

    @pl.loop(0, chunks)
    def _(c):
        tile_copy(tiles, buffer, sems, c).wait()
        base = c * CHUNK
        products = [
            jnp.dot(buffer[base + u], xs[cols[base + u]], preferred_element_type=jnp.float32)
            for u in range(CHUNK)
        ]
        for u in range(CHUNK):
            acc[rows[base + u]] += products[u]

    out[...] = acc[:ROWS].astype(jnp.bfloat16)


def backward_kernel(count, rows, cols, tiles, grads, own, other, buffer, acc, sems):
    chunks = (count[0] + CHUNK - 1) // CHUNK

    @pl.loop(0, chunks)
    def _(c):
        tile_copy(tiles, buffer, sems, c).start()

    acc[...] = jnp.zeros_like(acc)

    @pl.loop(0, chunks)
    def _(c):
        tile_copy(tiles, buffer, sems, c).wait()
        base = c * CHUNK
        products = [
            jnp.dot(grads[rows[base + u]], buffer[base + u], preferred_element_type=jnp.float32)
            for u in range(CHUNK)
        ]
        for u in range(CHUNK):
            acc[cols[base + u]] += products[u]

    own[...] = acc[:HALF]
    other[...] = acc[HALF:COLS].astype(jnp.bfloat16)


SMEM = pl.BlockSpec(memory_space=pltpu.SMEM)
VMEM = pl.BlockSpec(memory_space=pltpu.VMEM)
HBM = pl.BlockSpec(memory_space=pl.ANY)


def forward_pass(count, rows, cols, tiles, own, other):
    cap = tiles.shape[0]
    return pl.pallas_call(
        forward_kernel,
        out_shape=jax.ShapeDtypeStruct((ROWS, BLOCK, BLOCK), jnp.bfloat16),
        in_specs=[SMEM, SMEM, SMEM, HBM, HBM, HBM],
        out_specs=VMEM,
        scratch_shapes=[
            pltpu.VMEM((cap, BLOCK, BLOCK), jnp.bfloat16),
            pltpu.VMEM((COLS, BLOCK, BLOCK), jnp.bfloat16),
            pltpu.VMEM((ROWS + 1, BLOCK, BLOCK), jnp.float32),
            pltpu.SemaphoreType.DMA((cap // CHUNK,)),
            pltpu.SemaphoreType.DMA((2,)),
        ],
        compiler_params=pltpu.CompilerParams(vmem_limit_bytes=32 << 20),
        cost_estimate=pl.CostEstimate(flops=1 << 30, bytes_accessed=11 << 20, transcendentals=0),
        name="forward_tiles",
    )(count, rows, cols, tiles, own, other)


def backward_pass(count, rows, cols, tiles, grads):
    cap = tiles.shape[0]
    return pl.pallas_call(
        backward_kernel,
        out_shape=(
            jax.ShapeDtypeStruct((HALF, BLOCK, BLOCK), jnp.float32),
            jax.ShapeDtypeStruct((HALF, BLOCK, BLOCK), jnp.bfloat16),
        ),
        in_specs=[SMEM, SMEM, SMEM, HBM, VMEM],
        out_specs=(VMEM, VMEM),
        scratch_shapes=[
            pltpu.VMEM((cap, BLOCK, BLOCK), jnp.bfloat16),
            pltpu.VMEM((COLS + 1, BLOCK, BLOCK), jnp.float32),
            pltpu.SemaphoreType.DMA((cap // CHUNK,)),
        ],
        compiler_params=pltpu.CompilerParams(vmem_limit_bytes=32 << 20),
        cost_estimate=pl.CostEstimate(flops=1 << 30, bytes_accessed=12 << 20, transcendentals=0),
        name="backward_tiles",
    )(count, rows, cols, tiles, grads)


def spread(block, axes):
    n = lax.axis_size(axes)
    return lax.all_to_all(jnp.broadcast_to(block[None], (n, *block.shape)), axes, 0, 0)


def local(features, weight, cotangent, tiles, row_ids, col_ids, counts):
    x = features[0]
    nodes, feats = x.shape
    tiles = tiles[0, 0]
    cap = tiles.shape[0]
    count = counts[0]
    rows = row_ids[0, 0]
    core = lax.axis_index("core")

    cols = col_ids[0, 0]
    col_place = (((cols // 2) % 2) ^ core) * HALF + (cols // 4) * 2 + cols % 2
    valid = jnp.arange(cap, dtype=jnp.int32) < count[0]
    rows_into = jnp.where(valid, rows, ROWS)
    cols_into = jnp.where(valid, col_place, COLS)

    own_x = spread(x, COLUMN).reshape(HALF, BLOCK, feats)
    other_x = lax.ppermute(own_x, "core", SWAP)
    y_part = forward_pass(count, rows_into, col_place, tiles, own_x, other_x)

    reps = lax.axis_size(REP)
    y_parts = lax.all_to_all(y_part.reshape(reps, nodes, feats), REP, 0, 0)
    y = jnp.sum(y_parts.astype(jnp.float32), axis=0)
    z = jnp.dot(y, weight.astype(jnp.float32), precision=lax.Precision.HIGHEST)
    sigma = jax.nn.sigmoid(z)
    hidden = (z * sigma).astype(jnp.bfloat16)
    grad_pre = (
        cotangent[0].astype(jnp.float32) * sigma * (1.0 + z * (1.0 - sigma))
    ).astype(jnp.bfloat16)

    weight_part = lax.dot_general(
        y.astype(jnp.bfloat16), grad_pre, (((0,), (0,)), ((), ())),
        preferred_element_type=jnp.float32,
    ).astype(jnp.bfloat16).reshape(reps, feats // reps, feats)
    grad_t = jnp.swapaxes(grad_pre.reshape(nodes // BLOCK, BLOCK, feats), 1, 2)
    grad_t = grad_t.reshape(1, nodes, feats)
    sent = jnp.concatenate(
        [jnp.broadcast_to(grad_t, (reps, nodes, feats)), weight_part], axis=1
    )
    got = lax.all_to_all(sent, REP, 0, 0)
    grads = got[:, :nodes].reshape(ROWS, feats, BLOCK)
    weight_rep = jnp.sum(got[:, nodes:].astype(jnp.float32), axis=0)
    weight_chip = weight_rep + lax.ppermute(weight_rep, "core", SWAP)

    slab_own, slab_other = backward_pass(count, rows, cols_into, tiles, grads)
    slab_chip = slab_own + lax.ppermute(slab_other, "core", SWAP).astype(jnp.float32)
    peers = lax.axis_size(COLUMN)
    sent = jnp.concatenate(
        [
            slab_chip.astype(jnp.bfloat16).reshape(peers, nodes, feats),
            jnp.broadcast_to(
                weight_chip.astype(jnp.bfloat16)[None], (peers, *weight_chip.shape)
            ),
        ],
        axis=1,
    )
    got = lax.all_to_all(sent, COLUMN, 0, 0).astype(jnp.float32)
    total = jnp.sum(got, axis=0)
    grad_xw_t = total[:nodes].astype(jnp.bfloat16).reshape(nodes // BLOCK, feats, BLOCK)
    grad_feats = jnp.einsum(
        "hfn,kf->hnk", grad_xw_t, weight, preferred_element_type=jnp.float32
    ).astype(jnp.bfloat16)
    grad_weight = spread(total[nodes:], REP).reshape(feats, feats)
    return hidden[None], grad_feats.reshape(1, nodes, feats), grad_weight


def solution(mesh):
    mesh = Mesh(mesh.devices.reshape(SIZES), AXES)
    placed = P(ROW, REP)
    return jax.shard_map(
        local,
        mesh=mesh,
        in_specs=(placed, P(), placed, placed, placed, placed, placed),
        out_specs=(placed, placed, P()),
        check_vma=False,
    )
```

```python
import jax
import jax.numpy as jnp
from jax import lax
from jax.experimental import pallas as pl
from jax.experimental.pallas import tpu as pltpu
from jax.sharding import Mesh, PartitionSpec as P

CHUNK = 32
BLOCK = 128
ROWS = 16
COLS = 64
PART = COLS // 4
SPAN = PART * BLOCK
EXTRA = BLOCK // 2
SIZES = (4, 2, 2, 4, 2, 2)
AXES = ("x", "ylo", "yhi", "zq", "zp", "core")
REP = ("x", "ylo")
ROW = ("yhi", "zq", "zp", "core")
PARITY = ("yhi", "zq")
ALONG = ("zq", "zp", "core")
SWAP = ((0, 1), (1, 0))
NEXT = tuple((2 * z, 2 * ((z + 1) % 8)) for z in range(8)) + tuple(
    (2 * z + 1, 2 * ((z + 7) % 8) + 1) for z in range(8)
)


def tile_copy(tiles, buffer, sems, chunk):
    span = pl.ds(chunk * CHUNK, CHUNK)
    return pltpu.make_async_copy(tiles.at[span], buffer.at[span], sems.at[chunk])


def forward_kernel(count, rows, cols, tiles, x0, x1, x2, x3, out, buffer, xs, acc, sems, xsems):
    chunks = (count[0] + CHUNK - 1) // CHUNK
    moves = [
        pltpu.make_async_copy(source, xs.at[pl.ds(k * PART, PART)], xsems.at[k])
        for k, source in enumerate((x0, x1, x2, x3))
    ]
    for move in moves:
        move.start()

    @pl.loop(0, chunks)
    def _(c):
        tile_copy(tiles, buffer, sems, c).start()

    acc[...] = jnp.zeros_like(acc)
    for move in moves:
        move.wait()

    @pl.loop(0, chunks)
    def _(c):
        tile_copy(tiles, buffer, sems, c).wait()
        base = c * CHUNK
        products = [
            jnp.dot(buffer[base + u], xs[cols[base + u]], preferred_element_type=jnp.float32)
            for u in range(CHUNK)
        ]
        for u in range(CHUNK):
            acc[rows[base + u]] += products[u]

    out[...] = acc[:ROWS].astype(jnp.bfloat16)


def backward_kernel(
    count, core, rows, cols, tiles, got, own, other, buffer, acc, weight_sum, sems
):
    chunks = (count[0] + CHUNK - 1) // CHUNK

    @pl.loop(0, chunks)
    def _(c):
        tile_copy(tiles, buffer, sems, c).start()

    acc[...] = jnp.zeros_like(acc)
    reps = got.shape[0]
    nodes = got.shape[1] - BLOCK
    weight_sum[...] = sum(got[k, nodes:].astype(jnp.float32) for k in range(reps))

    @pl.loop(0, chunks)
    def _(c):
        tile_copy(tiles, buffer, sems, c).wait()
        base = c * CHUNK
        products = []
        for u in range(CHUNK):
            row = rows[base + u]
            grad = got[row // 2, pl.ds(pl.multiple_of((row % 2) * BLOCK, BLOCK), BLOCK), :]
            products.append(
                jnp.dot(grad, buffer[base + u], preferred_element_type=jnp.float32)
            )
        for u in range(CHUNK):
            acc[cols[base + u]] += products[u]

    feats = own.shape[1]
    mine = core[0]
    own[:SPAN] = acc[2 * PART : 3 * PART].reshape(SPAN, feats)
    own[SPAN : 2 * SPAN] = acc[:PART].reshape(SPAN, feats)
    own[2 * SPAN :] = weight_sum[pl.ds(pl.multiple_of(mine * EXTRA, EXTRA), EXTRA), :]
    other[:SPAN] = acc[3 * PART : 4 * PART].reshape(SPAN, feats).astype(jnp.bfloat16)
    other[SPAN : 2 * SPAN] = acc[PART : 2 * PART].reshape(SPAN, feats).astype(jnp.bfloat16)
    other[2 * SPAN :] = weight_sum[
        pl.ds(pl.multiple_of((1 - mine) * EXTRA, EXTRA), EXTRA), :
    ].astype(jnp.bfloat16)


def away_kernel(own, other, out):
    for at, to, size in ((0, 0, SPAN), (2 * SPAN, SPAN, EXTRA)):
        total = own[pl.ds(at, size), :] + other[pl.ds(at, size), :].astype(jnp.float32)
        out[pl.ds(to, size), :] = total.astype(jnp.bfloat16)


def home_kernel(own, other, came, out):
    peers = out.shape[0]
    nodes = out.shape[1] - EXTRA
    weight = (
        own[2 * SPAN :] + other[2 * SPAN :].astype(jnp.float32) + came[SPAN:].astype(jnp.float32)
    ).astype(jnp.bfloat16)
    for k in range(peers):
        here = pl.ds(SPAN + k * nodes, nodes)
        total = own[here, :] + other[here, :].astype(jnp.float32)
        total = total + came[pl.ds(k * nodes, nodes), :].astype(jnp.float32)
        out[k, :nodes] = total.astype(jnp.bfloat16)
        out[k, nodes:] = weight


SMEM = pl.BlockSpec(memory_space=pltpu.SMEM)
VMEM = pl.BlockSpec(memory_space=pltpu.VMEM)
ANY = pl.BlockSpec(memory_space=pl.ANY)


def forward_pass(count, rows, cols, tiles, parts):
    cap = tiles.shape[0]
    return pl.pallas_call(
        forward_kernel,
        out_shape=jax.ShapeDtypeStruct((ROWS, BLOCK, BLOCK), jnp.bfloat16),
        in_specs=[SMEM, SMEM, SMEM, ANY, ANY, ANY, ANY, ANY],
        out_specs=VMEM,
        scratch_shapes=[
            pltpu.VMEM((cap, BLOCK, BLOCK), jnp.bfloat16),
            pltpu.VMEM((COLS, BLOCK, BLOCK), jnp.bfloat16),
            pltpu.VMEM((ROWS + 1, BLOCK, BLOCK), jnp.float32),
            pltpu.SemaphoreType.DMA((cap // CHUNK,)),
            pltpu.SemaphoreType.DMA((4,)),
        ],
        compiler_params=pltpu.CompilerParams(vmem_limit_bytes=20 << 20),
        cost_estimate=pl.CostEstimate(flops=1 << 30, bytes_accessed=11 << 20, transcendentals=0),
        name="forward_tiles",
    )(count, rows, cols, pltpu.with_memory_space_constraint(tiles, pltpu.HBM), *parts)


def backward_pass(count, core, rows, cols, tiles, got):
    cap = tiles.shape[0]
    feats = got.shape[2]
    return pl.pallas_call(
        backward_kernel,
        out_shape=(
            jax.ShapeDtypeStruct((2 * SPAN + EXTRA, feats), jnp.float32),
            jax.ShapeDtypeStruct((2 * SPAN + EXTRA, feats), jnp.bfloat16),
        ),
        in_specs=[SMEM, SMEM, SMEM, SMEM, ANY, VMEM],
        out_specs=(VMEM, VMEM),
        scratch_shapes=[
            pltpu.VMEM((cap, BLOCK, BLOCK), jnp.bfloat16),
            pltpu.VMEM((COLS + 1, BLOCK, BLOCK), jnp.float32),
            pltpu.VMEM((BLOCK, BLOCK), jnp.float32),
            pltpu.SemaphoreType.DMA((cap // CHUNK,)),
        ],
        compiler_params=pltpu.CompilerParams(vmem_limit_bytes=20 << 20),
        cost_estimate=pl.CostEstimate(flops=1 << 30, bytes_accessed=12 << 20, transcendentals=0),
        name="backward_tiles",
    )(count, core, rows, cols, pltpu.with_memory_space_constraint(tiles, pltpu.HBM), got)


def merge(kernel, shape, *arrays):
    return pl.pallas_call(
        kernel,
        out_shape=jax.ShapeDtypeStruct(shape, jnp.bfloat16),
        in_specs=[VMEM] * len(arrays),
        out_specs=VMEM,
        compiler_params=pltpu.CompilerParams(vmem_limit_bytes=16 << 20),
        cost_estimate=pl.CostEstimate(flops=1 << 20, bytes_accessed=4 << 20, transcendentals=0),
        name=kernel.__name__,
    )(*arrays)


def spread(block, axes):
    n = lax.axis_size(axes)
    return lax.all_to_all(jnp.broadcast_to(block[None], (n, *block.shape)), axes, 0, 0)


def local(features, weight, cotangent, tiles, row_ids, col_ids, counts):
    x = features[0]
    nodes, feats = x.shape
    tiles = tiles[0, 0]
    cap = tiles.shape[0]
    count = counts[0]
    rows = row_ids[0, 0]
    core = lax.axis_index("core")

    cols = col_ids[0, 0]
    z = (cols // 4) % 8
    part = ((z % 2) ^ lax.axis_index("zp")) * 2 + (((cols // 2) % 2) ^ core)
    place = part * PART + ((cols // 32) * 4 + z // 2) * 2 + cols % 2
    valid = jnp.arange(cap, dtype=jnp.int32) < count[0]
    rows_into = jnp.where(valid, rows, ROWS)
    place_into = jnp.where(valid, place, COLS)

    own = spread(x, PARITY)
    beside = lax.ppermute(own, ALONG, NEXT)
    own_other = lax.ppermute(own, "core", SWAP)
    beside_other = lax.ppermute(beside, "core", SWAP)
    parts = [p.reshape(PART, BLOCK, feats) for p in (own, own_other, beside, beside_other)]
    y_part = forward_pass(count, rows_into, place, tiles, parts)

    reps = lax.axis_size(REP)
    y_parts = lax.all_to_all(y_part.reshape(reps, nodes, feats), REP, 0, 0)
    y = jnp.sum(y_parts.astype(jnp.float32), axis=0)
    z = jnp.dot(y, weight.astype(jnp.float32), precision=lax.Precision.HIGHEST)
    sigma = jax.nn.sigmoid(z)
    hidden = (z * sigma).astype(jnp.bfloat16)
    grad_pre = (
        cotangent[0].astype(jnp.float32) * sigma * (1.0 + z * (1.0 - sigma))
    ).astype(jnp.bfloat16)

    weight_part = lax.dot_general(
        y.astype(jnp.bfloat16), grad_pre, (((0,), (0,)), ((), ())),
        preferred_element_type=jnp.float32,
    ).astype(jnp.bfloat16)
    grad_t = jnp.swapaxes(grad_pre.reshape(nodes // BLOCK, BLOCK, feats), 1, 2)
    got = spread(jnp.concatenate([grad_t.reshape(nodes, feats), weight_part]), REP)

    slab_own, slab_other = backward_pass(count, core[None], rows, place_into, tiles, got)
    slab_other = lax.ppermute(slab_other, "core", SWAP)
    away = merge(away_kernel, (SPAN + EXTRA, feats), slab_own, slab_other)
    came = lax.ppermute(away, ALONG, NEXT)
    peers = lax.axis_size(PARITY)
    sent = merge(home_kernel, (peers, nodes + EXTRA, feats), slab_own, slab_other, came)
    got = lax.all_to_all(sent, PARITY, 0, 0)
    total = jnp.sum(got.astype(jnp.float32), axis=0)
    grad_xw_t = total[:nodes].astype(jnp.bfloat16).reshape(nodes // BLOCK, feats, BLOCK)
    grad_feats = jnp.einsum(
        "hfn,kf->hnk", grad_xw_t, weight, preferred_element_type=jnp.float32
    ).astype(jnp.bfloat16)
    mine = total[nodes:]
    theirs = lax.ppermute(mine, "core", SWAP)
    grad_weight = jnp.where(
        core == 0, jnp.concatenate([mine, theirs]), jnp.concatenate([theirs, mine])
    )
    return hidden[None], grad_feats.reshape(1, nodes, feats), grad_weight


def solution(mesh):
    mesh = Mesh(mesh.devices.reshape(SIZES), AXES)
    placed = P(ROW, REP)
    return jax.shard_map(
        local,
        mesh=mesh,
        in_specs=(placed, P(), placed, placed, placed, placed, placed),
        out_specs=(placed, placed, P()),
        check_vma=False,
    )
```

```python
import functools

import jax
import jax.numpy as jnp
from jax import lax
from jax.experimental import pallas as pl
from jax.experimental.pallas import tpu as pltpu
from jax.sharding import Mesh, PartitionSpec as P

CHUNK = 32
BLOCK = 128
ROWS = 16
PLACES = 32
PART = PLACES // 2
ROW_AT, PLACE_AT = 8, 13
SPARE = (ROWS << ROW_AT) | (PLACES << PLACE_AT)
SPAN = PART * BLOCK
EXTRA = BLOCK // 2
SIZES = (4, 2, 2, 4, 2, 2)
AXES = ("x", "ylo", "yhi", "zq", "zp", "core")
REP = ("x", "ylo")
ROW = ("yhi", "zq", "zp", "core")
PARITY = ("yhi", "zq")
ALONG = ("zq", "zp", "core")
SWAP = ((0, 1), (1, 0))
NEXT = tuple((2 * z, 2 * ((z + 1) % 8)) for z in range(8)) + tuple(
    (2 * z + 1, 2 * ((z + 7) % 8) + 1) for z in range(8)
)


def tile_copy(tiles, buffer, sems, chunk):
    span = pl.ds(chunk * CHUNK, CHUNK)
    return pltpu.make_async_copy(tiles.at[span], buffer.at[span], sems.at[chunk])


def tile_groups(part, counts, lists, group, ready):
    count = counts[part]

    def step(k, done):
        base = k * CHUNK
        last = lists[part, jnp.minimum(base + CHUNK, count) - 1] & 255
        done = ready(done, last // CHUNK + 1)
        group([lists[part, base + u] for u in range(CHUNK)])
        return done

    return lax.fori_loop(0, (count + CHUNK - 1) // CHUNK, step, 0)


def forward_kernel(part, counts, lists, tiles, *rest):
    if part == 0:
        x0, x1, out, buffer, xs, acc, xsems, sems = rest
    else:
        before, x0, x1, out, xs, acc, xsems = rest
        buffer = tiles
    chunks = (counts[0] + counts[1] + CHUNK - 1) // CHUNK
    moves = [
        pltpu.make_async_copy(source, xs.at[pl.ds(k * PART, PART)], xsems.at[k])
        for k, source in enumerate((x0, x1))
    ]
    for move in moves:
        move.start()
    if part == 0:

        @pl.loop(0, chunks)
        def _(c):
            tile_copy(tiles, buffer, sems, c).start()

        acc[...] = jnp.zeros_like(acc)
    else:
        acc[:ROWS] = before[...]
    for move in moves:
        move.wait()

    def ready(done, need):
        if part == 0:

            @pl.loop(done, need)
            def _(c):
                tile_copy(tiles, buffer, sems, c).wait()

        return need

    def group(codes):
        products = [
            jnp.dot(
                buffer[code & 255],
                xs[(code >> PLACE_AT) & (PLACES - 1)],
                preferred_element_type=jnp.float32,
            )
            for code in codes
        ]
        for code, product in zip(codes, products):
            acc[(code >> ROW_AT) & 31] += product

    done = tile_groups(part, counts, lists, group, ready)
    ready(done, chunks)
    out[...] = acc[:ROWS].astype(out.dtype)


def backward_kernel(part, counts, core, lists, tiles, got, own, other, buffer, acc, *rest):
    weight_sum, sems = rest if part == 1 else (None, *rest)
    last = lists[part, jnp.maximum(counts[part], 1) - 1] & 255
    chunks = jnp.where(counts[part] > 0, last // CHUNK + 1, 0)

    @pl.loop(0, chunks)
    def _(c):
        tile_copy(tiles, buffer, sems, c).start()

    acc[...] = jnp.zeros_like(acc)
    nodes = got.shape[1] - BLOCK
    if part == 1:
        reps = got.shape[0]
        weight_sum[...] = sum(got[k, nodes:].astype(jnp.float32) for k in range(reps))

    def ready(done, need):
        @pl.loop(done, need)
        def _(c):
            tile_copy(tiles, buffer, sems, c).wait()

        return need

    def group(codes):
        products = []
        for code in codes:
            row = (code >> ROW_AT) & (ROWS - 1)
            grad = got[row // 2, pl.ds(pl.multiple_of((row % 2) * BLOCK, BLOCK), BLOCK), :]
            products.append(
                jnp.dot(grad, buffer[code & 255], preferred_element_type=jnp.float32)
            )
        for code, product in zip(codes, products):
            acc[code >> PLACE_AT] += product

    tile_groups(part, counts, lists, group, ready)
    feats = own.shape[1]
    own[:SPAN] = acc[:PART].reshape(SPAN, feats)
    other[:SPAN] = acc[PART:PLACES].reshape(SPAN, feats).astype(jnp.bfloat16)
    if part == 1:
        mine = pl.multiple_of(core[0] * EXTRA, EXTRA)
        theirs = pl.multiple_of((1 - core[0]) * EXTRA, EXTRA)
        own[SPAN:] = weight_sum[pl.ds(mine, EXTRA), :]
        other[SPAN:] = weight_sum[pl.ds(theirs, EXTRA), :].astype(jnp.bfloat16)


def away_kernel(own, other, out):
    out[...] = (own[...] + other[...].astype(jnp.float32)).astype(jnp.bfloat16)


def home_kernel(own, other, away_own, away_other, came, out):
    peers = out.shape[0]
    nodes = out.shape[1] - EXTRA
    weight = away_own[SPAN:] + away_other[SPAN:].astype(jnp.float32)
    weight = (weight + came[SPAN:].astype(jnp.float32)).astype(jnp.bfloat16)
    for k in range(peers):
        here = pl.ds(k * nodes, nodes)
        total = own[here, :] + other[here, :].astype(jnp.float32)
        total = total + came[here, :].astype(jnp.float32)
        out[k, :nodes] = total.astype(jnp.bfloat16)
        out[k, nodes:] = weight


SMEM = pl.BlockSpec(memory_space=pltpu.SMEM)
VMEM = pl.BlockSpec(memory_space=pltpu.VMEM)
ANY = pl.BlockSpec(memory_space=pl.ANY)


def forward_pass(part, counts, lists, tiles, parts, before=()):
    cap = tiles.shape[0]
    out = jax.ShapeDtypeStruct(
        (ROWS, BLOCK, BLOCK), jnp.float32 if part == 0 else jnp.bfloat16
    )
    scratch = [
        pltpu.VMEM((PLACES, BLOCK, BLOCK), jnp.bfloat16),
        pltpu.VMEM((ROWS + 1, BLOCK, BLOCK), jnp.float32),
        pltpu.SemaphoreType.DMA((2,)),
    ]
    if part == 0:
        scratch.append(pltpu.SemaphoreType.DMA((cap // CHUNK,)))
    return pl.pallas_call(
        functools.partial(forward_kernel, part),
        out_shape=(out, pltpu.VMEM((cap, BLOCK, BLOCK), jnp.bfloat16)) if part == 0 else out,
        in_specs=[SMEM, SMEM, ANY if part == 0 else VMEM] + [VMEM] * len(before) + [ANY, ANY],
        out_specs=(VMEM, VMEM) if part == 0 else VMEM,
        scratch_shapes=scratch,
        compiler_params=pltpu.CompilerParams(vmem_limit_bytes=20 << 20),
        cost_estimate=pl.CostEstimate(flops=1 << 30, bytes_accessed=9 << 20, transcendentals=0),
        name=f"forward_tiles_{part}",
    )(
        counts,
        lists,
        pltpu.with_memory_space_constraint(tiles, pltpu.HBM if part == 0 else pltpu.VMEM),
        *before,
        *parts,
    )


def backward_pass(part, counts, core, lists, tiles, got):
    cap = tiles.shape[0]
    feats = got.shape[2]
    size = SPAN + EXTRA * part
    scratch = [
        pltpu.VMEM((cap, BLOCK, BLOCK), jnp.bfloat16),
        pltpu.VMEM((PLACES + 1, BLOCK, BLOCK), jnp.float32),
        pltpu.SemaphoreType.DMA((cap // CHUNK,)),
    ]
    if part == 1:
        scratch.insert(2, pltpu.VMEM((BLOCK, BLOCK), jnp.float32))
    return pl.pallas_call(
        functools.partial(backward_kernel, part),
        out_shape=(
            jax.ShapeDtypeStruct((size, feats), jnp.float32),
            jax.ShapeDtypeStruct((size, feats), jnp.bfloat16),
        ),
        in_specs=[SMEM, SMEM, SMEM, ANY, VMEM],
        out_specs=(VMEM, VMEM),
        scratch_shapes=scratch,
        compiler_params=pltpu.CompilerParams(vmem_limit_bytes=20 << 20),
        cost_estimate=pl.CostEstimate(flops=1 << 30, bytes_accessed=9 << 20, transcendentals=0),
        name=f"backward_tiles_{part}",
    )(counts, core, lists, pltpu.with_memory_space_constraint(tiles, pltpu.HBM), got)


def merge(kernel, shape, *arrays):
    return pl.pallas_call(
        kernel,
        out_shape=jax.ShapeDtypeStruct(shape, jnp.bfloat16),
        in_specs=[VMEM] * len(arrays),
        out_specs=VMEM,
        compiler_params=pltpu.CompilerParams(vmem_limit_bytes=16 << 20),
        cost_estimate=pl.CostEstimate(flops=1 << 20, bytes_accessed=4 << 20, transcendentals=0),
        name=kernel.__name__,
    )(*arrays)


def spread(block, axes):
    n = lax.axis_size(axes)
    return lax.all_to_all(jnp.broadcast_to(block[None], (n, *block.shape)), axes, 0, 0)


def tile_lists(rows, cols, count, parity, core):
    slots = jnp.arange(rows.shape[0], dtype=jnp.int32)
    z = (cols // 4) % 8
    part = (z % 2) ^ parity
    place = (((cols // 2) % 2) ^ core) * PART + ((cols // 32) * 4 + z // 2) * 2 + cols % 2
    code = slots | (rows << ROW_AT) | (place << PLACE_AT)
    part = jnp.where(slots < count, part, 2)
    earlier = (slots[None, :] < slots[:, None]) & (part[None, :] == part[:, None])
    rank = jnp.sum(earlier.astype(jnp.int32), axis=1)
    parts = jnp.arange(2, dtype=jnp.int32)[:, None]
    mine = part[None, :] == parts
    hit = mine[:, None, :] & (rank[None, None, :] == slots[None, :, None])
    lists = SPARE + jnp.sum(jnp.where(hit, code - SPARE, 0), axis=2)
    return jnp.sum(mine.astype(jnp.int32), axis=1), lists


def local(features, weight, cotangent, tiles, row_ids, col_ids, counts):
    x = features[0]
    nodes, feats = x.shape
    tiles = tiles[0, 0]
    core = lax.axis_index("core")
    counts, lists = tile_lists(
        row_ids[0, 0], col_ids[0, 0], counts[0, 0], lax.axis_index("zp"), core
    )
    blocks = (PART, BLOCK, feats)

    own = spread(x, PARITY)
    beside = lax.ppermute(own, ALONG, NEXT)
    own_other = lax.ppermute(own, "core", SWAP)
    y_part, held = forward_pass(
        0, counts, lists, tiles, (own.reshape(blocks), own_other.reshape(blocks))
    )
    beside, y_part = lax.optimization_barrier((beside, y_part))
    beside_other = lax.ppermute(beside, "core", SWAP)
    y_part = forward_pass(
        1, counts, lists, held, (beside.reshape(blocks), beside_other.reshape(blocks)), (y_part,)
    )

    reps = lax.axis_size(REP)
    y_parts = lax.all_to_all(y_part.reshape(reps, nodes, feats), REP, 0, 0)
    y = jnp.sum(y_parts.astype(jnp.float32), axis=0)
    z = jnp.dot(y, weight.astype(jnp.float32), precision=lax.Precision.HIGHEST)
    sigma = jax.nn.sigmoid(z)
    hidden = (z * sigma).astype(jnp.bfloat16)
    grad_pre = (
        cotangent[0].astype(jnp.float32) * sigma * (1.0 + z * (1.0 - sigma))
    ).astype(jnp.bfloat16)

    weight_part = lax.dot_general(
        y.astype(jnp.bfloat16), grad_pre, (((0,), (0,)), ((), ())),
        preferred_element_type=jnp.float32,
    ).astype(jnp.bfloat16)
    grad_t = jnp.swapaxes(grad_pre.reshape(nodes // BLOCK, BLOCK, feats), 1, 2)
    got = spread(jnp.concatenate([grad_t.reshape(nodes, feats), weight_part]), REP)

    core_id = core[None]
    away_own, away_other = backward_pass(1, counts, core_id, lists, tiles, got)
    away_other = lax.ppermute(away_other, "core", SWAP)
    away = merge(away_kernel, away_own.shape, away_own, away_other)
    core_id, away = lax.optimization_barrier((core_id, away))
    came = lax.ppermute(away, ALONG, NEXT)
    home_own, home_other = backward_pass(0, counts, core_id, lists, tiles, got)
    home_other = lax.ppermute(home_other, "core", SWAP)
    peers = lax.axis_size(PARITY)
    sent = merge(
        home_kernel, (peers, nodes + EXTRA, feats), home_own, home_other, away_own, away_other, came
    )
    got = lax.all_to_all(sent, PARITY, 0, 0)
    total = jnp.sum(got.astype(jnp.float32), axis=0)
    grad_xw_t = total[:nodes].astype(jnp.bfloat16).reshape(nodes // BLOCK, feats, BLOCK)
    grad_feats = jnp.einsum(
        "hfn,kf->hnk", grad_xw_t, weight, preferred_element_type=jnp.float32
    ).astype(jnp.bfloat16)
    mine = total[nodes:]
    theirs = lax.ppermute(mine, "core", SWAP)
    grad_weight = jnp.where(
        core == 0, jnp.concatenate([mine, theirs]), jnp.concatenate([theirs, mine])
    )
    return hidden[None], grad_feats.reshape(1, nodes, feats), grad_weight


def solution(mesh):
    mesh = Mesh(mesh.devices.reshape(SIZES), AXES)
    placed = P(ROW, REP)
    return jax.shard_map(
        local,
        mesh=mesh,
        in_specs=(placed, P(), placed, placed, placed, placed, placed),
        out_specs=(placed, placed, P()),
        check_vma=False,
    )
```

```python
import functools

import jax
import jax.numpy as jnp
from jax import lax
from jax.experimental import pallas as pl
from jax.experimental.pallas import tpu as pltpu
from jax.sharding import Mesh, PartitionSpec as P

CHUNK = 32
BLOCK = 128
ROWS = 16
PLACES = 32
PART = PLACES // 2
ROW_AT, PLACE_AT = 8, 13
SPARE = (ROWS << ROW_AT) | (PLACES << PLACE_AT)
SPAN = PART * BLOCK
EXTRA = BLOCK // 2
SIZES = (4, 2, 2, 4, 2, 2)
AXES = ("x", "ylo", "yhi", "zq", "zp", "core")
REP = ("x", "ylo")
ROW = ("yhi", "zq", "zp", "core")
PARITY = ("yhi", "zq")
ALONG = ("zq", "zp", "core")
SWAP = ((0, 1), (1, 0))
NEXT = tuple((2 * z, 2 * ((z + 1) % 8)) for z in range(8)) + tuple(
    (2 * z + 1, 2 * ((z + 7) % 8) + 1) for z in range(8)
)


def tile_copy(tiles, buffer, sems, chunk):
    span = pl.ds(chunk * CHUNK, CHUNK)
    return pltpu.make_async_copy(tiles.at[span], buffer.at[span], sems.at[chunk])


def tile_groups(part, counts, lists, group, ready):
    count = counts[part]

    def step(k, done):
        base = k * CHUNK
        last = lists[part, jnp.minimum(base + CHUNK, count) - 1] & 255
        done = ready(done, last // CHUNK + 1)
        group([lists[part, base + u] for u in range(CHUNK)])
        return done

    return lax.fori_loop(0, (count + CHUNK - 1) // CHUNK, step, 0)


def forward_kernel(part, counts, lists, tiles, *rest):
    if part == 0:
        x0, x1, out, buffer, xs, acc, xsems, sems = rest
    else:
        before, x0, x1, out, xs, acc, xsems = rest
        buffer = tiles
    chunks = (counts[0] + counts[1] + CHUNK - 1) // CHUNK
    moves = [
        pltpu.make_async_copy(source, xs.at[pl.ds(k * PART, PART)], xsems.at[k])
        for k, source in enumerate((x0, x1))
    ]
    for move in moves:
        move.start()
    if part == 0:

        @pl.loop(0, chunks)
        def _(c):
            tile_copy(tiles, buffer, sems, c).start()

        acc[...] = jnp.zeros_like(acc)
    else:
        acc[:ROWS] = before[...]
    for move in moves:
        move.wait()

    def ready(done, need):
        if part == 0:

            @pl.loop(done, need)
            def _(c):
                tile_copy(tiles, buffer, sems, c).wait()

        return need

    def group(codes):
        products = [
            jnp.dot(
                buffer[code & 255],
                xs[(code >> PLACE_AT) & (PLACES - 1)],
                preferred_element_type=jnp.float32,
            )
            for code in codes
        ]
        for code, product in zip(codes, products):
            acc[(code >> ROW_AT) & 31] += product

    done = tile_groups(part, counts, lists, group, ready)
    ready(done, chunks)
    out[...] = acc[:ROWS].astype(out.dtype)


def backward_kernel(part, counts, core, lists, buffer, got, own, other, acc, weight_sum=None):
    acc[...] = jnp.zeros_like(acc)
    nodes = got.shape[1] - BLOCK
    if part == 1:
        reps = got.shape[0]
        weight_sum[...] = sum(got[k, nodes:].astype(jnp.float32) for k in range(reps))

    def group(codes):
        products = []
        for code in codes:
            row = (code >> ROW_AT) & (ROWS - 1)
            grad = got[row // 2, pl.ds(pl.multiple_of((row % 2) * BLOCK, BLOCK), BLOCK), :]
            products.append(
                jnp.dot(grad, buffer[code & 255], preferred_element_type=jnp.float32)
            )
        for code, product in zip(codes, products):
            acc[code >> PLACE_AT] += product

    tile_groups(part, counts, lists, group, lambda done, need: need)
    feats = own.shape[1]
    own[:SPAN] = acc[:PART].reshape(SPAN, feats)
    other[:SPAN] = acc[PART:PLACES].reshape(SPAN, feats).astype(jnp.bfloat16)
    if part == 1:
        mine = pl.multiple_of(core[0] * EXTRA, EXTRA)
        theirs = pl.multiple_of((1 - core[0]) * EXTRA, EXTRA)
        own[SPAN:] = weight_sum[pl.ds(mine, EXTRA), :]
        other[SPAN:] = weight_sum[pl.ds(theirs, EXTRA), :].astype(jnp.bfloat16)


def middle_kernel(y_parts, weight, cotangent, hidden, sent):
    reps, nodes, feats = y_parts.shape
    y = sum(y_parts[k].astype(jnp.float32) for k in range(reps))
    z = jnp.dot(
        y,
        weight[...].astype(jnp.float32),
        precision=lax.Precision.HIGHEST,
        preferred_element_type=jnp.float32,
    )
    sigma = jax.nn.sigmoid(z)
    hidden[...] = (z * sigma).astype(jnp.bfloat16)
    grad = cotangent[...].astype(jnp.float32) * sigma * (1.0 + z * (1.0 - sigma))
    weight_part = jnp.dot(
        y.T.astype(jnp.bfloat16), grad.astype(jnp.bfloat16), preferred_element_type=jnp.float32
    ).astype(jnp.bfloat16)
    for at in range(0, nodes, BLOCK):
        grad_t = grad[at : at + BLOCK].T.astype(jnp.bfloat16)
        for k in range(reps):
            sent[k, pl.ds(at, BLOCK), :] = grad_t
    for k in range(reps):
        sent[k, nodes:] = weight_part


def away_kernel(own, other, out):
    out[...] = (own[...] + other[...].astype(jnp.float32)).astype(jnp.bfloat16)


def home_kernel(own, other, away_own, away_other, came, out):
    peers = out.shape[0]
    nodes = out.shape[1] - EXTRA
    weight = away_own[SPAN:] + away_other[SPAN:].astype(jnp.float32)
    weight = (weight + came[SPAN:].astype(jnp.float32)).astype(jnp.bfloat16)
    for k in range(peers):
        here = pl.ds(k * nodes, nodes)
        total = own[here, :] + other[here, :].astype(jnp.float32)
        total = total + came[here, :].astype(jnp.float32)
        out[k, :nodes] = total.astype(jnp.bfloat16)
        out[k, nodes:] = weight


def end_kernel(got, weight, grad_feats, weight_rows):
    total = sum(got[k].astype(jnp.float32) for k in range(got.shape[0]))
    nodes = grad_feats.shape[0]
    for at in range(0, nodes, BLOCK):
        grad_xw = total[at : at + BLOCK].T.astype(jnp.bfloat16)
        grad_feats[pl.ds(at, BLOCK), :] = lax.dot_general(
            grad_xw, weight[...], (((1,), (1,)), ((), ())), preferred_element_type=jnp.float32
        ).astype(jnp.bfloat16)
    weight_rows[...] = total[nodes:]


SMEM = pl.BlockSpec(memory_space=pltpu.SMEM)
VMEM = pl.BlockSpec(memory_space=pltpu.VMEM)
ANY = pl.BlockSpec(memory_space=pl.ANY)


def forward_pass(part, counts, lists, tiles, parts, before=()):
    cap = tiles.shape[0]
    out = jax.ShapeDtypeStruct(
        (ROWS, BLOCK, BLOCK), jnp.float32 if part == 0 else jnp.bfloat16
    )
    scratch = [
        pltpu.VMEM((PLACES, BLOCK, BLOCK), jnp.bfloat16),
        pltpu.VMEM((ROWS + 1, BLOCK, BLOCK), jnp.float32),
        pltpu.SemaphoreType.DMA((2,)),
    ]
    if part == 0:
        scratch.append(pltpu.SemaphoreType.DMA((cap // CHUNK,)))
    return pl.pallas_call(
        functools.partial(forward_kernel, part),
        out_shape=(out, pltpu.VMEM((cap, BLOCK, BLOCK), jnp.bfloat16)) if part == 0 else out,
        in_specs=[SMEM, SMEM, ANY if part == 0 else VMEM] + [VMEM] * len(before) + [ANY, ANY],
        out_specs=(VMEM, VMEM) if part == 0 else VMEM,
        scratch_shapes=scratch,
        compiler_params=pltpu.CompilerParams(vmem_limit_bytes=20 << 20),
        cost_estimate=pl.CostEstimate(flops=1 << 30, bytes_accessed=9 << 20, transcendentals=0),
        name=f"forward_tiles_{part}",
    )(
        counts,
        lists,
        pltpu.with_memory_space_constraint(tiles, pltpu.HBM if part == 0 else pltpu.VMEM),
        *before,
        *parts,
    )


def backward_pass(part, counts, core, lists, held, got):
    feats = got.shape[2]
    size = SPAN + EXTRA * part
    scratch = [pltpu.VMEM((PLACES + 1, BLOCK, BLOCK), jnp.float32)]
    if part == 1:
        scratch.append(pltpu.VMEM((BLOCK, BLOCK), jnp.float32))
    return pl.pallas_call(
        functools.partial(backward_kernel, part),
        out_shape=(
            jax.ShapeDtypeStruct((size, feats), jnp.float32),
            jax.ShapeDtypeStruct((size, feats), jnp.bfloat16),
        ),
        in_specs=[SMEM, SMEM, SMEM, VMEM, VMEM],
        out_specs=(VMEM, VMEM),
        scratch_shapes=scratch,
        compiler_params=pltpu.CompilerParams(vmem_limit_bytes=20 << 20),
        cost_estimate=pl.CostEstimate(flops=1 << 30, bytes_accessed=1 << 20, transcendentals=0),
        name=f"backward_tiles_{part}",
    )(counts, core, lists, pltpu.with_memory_space_constraint(held, pltpu.VMEM), got)


def merge(kernel, out_shape, *arrays):
    out_specs = (VMEM,) * len(out_shape) if isinstance(out_shape, tuple) else VMEM
    return pl.pallas_call(
        kernel,
        out_shape=out_shape,
        in_specs=[VMEM] * len(arrays),
        out_specs=out_specs,
        compiler_params=pltpu.CompilerParams(vmem_limit_bytes=16 << 20),
        cost_estimate=pl.CostEstimate(flops=1 << 20, bytes_accessed=4 << 20, transcendentals=0),
        name=kernel.__name__,
    )(*arrays)


def spread(block, axes):
    n = lax.axis_size(axes)
    return lax.all_to_all(jnp.broadcast_to(block[None], (n, *block.shape)), axes, 0, 0)


def tile_lists(rows, cols, count, parity, core):
    slots = jnp.arange(rows.shape[0], dtype=jnp.int32)
    z = (cols // 4) % 8
    part = (z % 2) ^ parity
    place = (((cols // 2) % 2) ^ core) * PART + ((cols // 32) * 4 + z // 2) * 2 + cols % 2
    code = slots | (rows << ROW_AT) | (place << PLACE_AT)
    part = jnp.where(slots < count, part, 2)
    earlier = (slots[None, :] < slots[:, None]) & (part[None, :] == part[:, None])
    rank = jnp.sum(earlier.astype(jnp.int32), axis=1)
    parts = jnp.arange(2, dtype=jnp.int32)[:, None]
    mine = part[None, :] == parts
    hit = mine[:, None, :] & (rank[None, None, :] == slots[None, :, None])
    lists = SPARE + jnp.sum(jnp.where(hit, code - SPARE, 0), axis=2)
    return jnp.sum(mine.astype(jnp.int32), axis=1), lists


def local(features, weight, cotangent, tiles, row_ids, col_ids, counts):
    x = features[0]
    nodes, feats = x.shape
    tiles = tiles[0, 0]
    core = lax.axis_index("core")
    counts, lists = tile_lists(
        row_ids[0, 0], col_ids[0, 0], counts[0, 0], lax.axis_index("zp"), core
    )
    blocks = (PART, BLOCK, feats)

    own = spread(x, PARITY)
    beside = lax.ppermute(own, ALONG, NEXT)
    own_other = lax.ppermute(own, "core", SWAP)
    y_part, held = forward_pass(
        0, counts, lists, tiles, (own.reshape(blocks), own_other.reshape(blocks))
    )
    beside, y_part = lax.optimization_barrier((beside, y_part))
    beside_other = lax.ppermute(beside, "core", SWAP)
    y_part = forward_pass(
        1, counts, lists, held, (beside.reshape(blocks), beside_other.reshape(blocks)), (y_part,)
    )

    reps = lax.axis_size(REP)
    y_parts = lax.all_to_all(y_part.reshape(reps, nodes, feats), REP, 0, 0)
    hidden, sent = pl.pallas_call(
        middle_kernel,
        out_shape=(
            jax.ShapeDtypeStruct((nodes, feats), jnp.bfloat16),
            pltpu.VMEM((reps, nodes + feats, feats), jnp.bfloat16),
        ),
        in_specs=[VMEM, VMEM, VMEM],
        out_specs=(VMEM, VMEM),
        compiler_params=pltpu.CompilerParams(vmem_limit_bytes=16 << 20),
        cost_estimate=pl.CostEstimate(flops=1 << 25, bytes_accessed=4 << 20, transcendentals=1 << 15),
        name="middle",
    )(y_parts, weight, cotangent[0])
    got = lax.all_to_all(sent, REP, 0, 0)
    away_own, away_other = backward_pass(1, counts, core[None], lists, held, got)
    away_other = lax.ppermute(away_other, "core", SWAP)
    away = merge(
        away_kernel, jax.ShapeDtypeStruct(away_own.shape, jnp.bfloat16), away_own, away_other
    )
    counts, away = lax.optimization_barrier((counts, away))
    came = lax.ppermute(away, ALONG, NEXT)
    home_own, home_other = backward_pass(0, counts, core[None], lists, held, got)
    home_other = lax.ppermute(home_other, "core", SWAP)
    peers = lax.axis_size(PARITY)
    sent = merge(
        home_kernel,
        pltpu.VMEM((peers, nodes + EXTRA, feats), jnp.bfloat16),
        home_own, home_other, away_own, away_other, came,
    )
    got = lax.all_to_all(sent, PARITY, 0, 0)
    grad_feats, mine = merge(
        end_kernel,
        (
            jax.ShapeDtypeStruct((nodes, feats), jnp.bfloat16),
            jax.ShapeDtypeStruct((EXTRA, feats), jnp.float32),
        ),
        got, weight,
    )
    theirs = lax.ppermute(mine, "core", SWAP)
    grad_weight = jnp.where(
        core == 0, jnp.concatenate([mine, theirs]), jnp.concatenate([theirs, mine])
    )
    return hidden[None], grad_feats.reshape(1, nodes, feats), grad_weight


def solution(mesh):
    mesh = Mesh(mesh.devices.reshape(SIZES), AXES)
    placed = P(ROW, REP)
    return jax.shard_map(
        local,
        mesh=mesh,
        in_specs=(placed, P(), placed, placed, placed, placed, placed),
        out_specs=(placed, placed, P()),
        check_vma=False,
    )
```

```python
import functools

import jax
import jax.numpy as jnp
from jax import lax
from jax.experimental import pallas as pl
from jax.experimental.pallas import tpu as pltpu
from jax.sharding import Mesh, PartitionSpec as P

CHUNK = 32
BLOCK = 128
ROWS = 16
PLACES = 32
PART = PLACES // 2
ROW_AT, PLACE_AT = 8, 13
SPARE = (ROWS << ROW_AT) | (PLACES << PLACE_AT)
CAP = 256
COUNT_AT = CAP
WIDTH = CAP + 128
SPAN = PART * BLOCK
EXTRA = BLOCK // 2
SIZES = (4, 2, 2, 4, 2, 2)
AXES = ("x", "ylo", "yhi", "zq", "zp", "core")
REP = ("x", "ylo")
ROW = ("yhi", "zq", "zp", "core")
PARITY = ("yhi", "zq")
ALONG = ("zq", "zp", "core")
SWAP = ((0, 1), (1, 0))
NEXT = tuple((2 * z, 2 * ((z + 1) % 8)) for z in range(8)) + tuple(
    (2 * z + 1, 2 * ((z + 7) % 8) + 1) for z in range(8)
)


def tile_copy(tiles, buffer, sems, chunk):
    span = pl.ds(chunk * CHUNK, CHUNK)
    return pltpu.make_async_copy(tiles.at[span], buffer.at[span], sems.at[chunk])


def tile_groups(part, lists, group, ready):
    count = lists[part, COUNT_AT]

    def step(k, done):
        base = k * CHUNK
        last = lists[part, jnp.minimum(base + CHUNK, count) - 1] & 255
        done = ready(done, last // CHUNK + 1)
        group([lists[part, base + u] for u in range(CHUNK)])
        return done

    return lax.fori_loop(0, (count + CHUNK - 1) // CHUNK, step, 0)


def forward_kernel(part, lists, tiles, *rest):
    if part == 0:
        x0, x1, out, buffer, xs, acc, xsems, sems = rest
    else:
        before, x0, x1, out, xs, acc, xsems = rest
        buffer = tiles
    chunks = (lists[0, COUNT_AT] + lists[1, COUNT_AT] + CHUNK - 1) // CHUNK
    moves = [
        pltpu.make_async_copy(source, xs.at[pl.ds(k * PART, PART)], xsems.at[k])
        for k, source in enumerate((x0, x1))
    ]
    for move in moves:
        move.start()
    if part == 0:

        @pl.loop(0, chunks)
        def _(c):
            tile_copy(tiles, buffer, sems, c).start()

        acc[...] = jnp.zeros_like(acc)
    else:
        acc[:ROWS] = before[...]
    for move in moves:
        move.wait()

    def ready(done, need):
        if part == 0:

            @pl.loop(done, need)
            def _(c):
                tile_copy(tiles, buffer, sems, c).wait()

        return need

    def group(codes):
        products = [
            jnp.dot(
                buffer[code & 255],
                xs[(code >> PLACE_AT) & (PLACES - 1)],
                preferred_element_type=jnp.float32,
            )
            for code in codes
        ]
        for code, product in zip(codes, products):
            acc[(code >> ROW_AT) & 31] += product

    done = tile_groups(part, lists, group, ready)
    ready(done, chunks)
    out[...] = acc[:ROWS].astype(out.dtype)


def backward_kernel(part, lists, buffer, got, own, other, acc, weight_sum=None):
    acc[...] = jnp.zeros_like(acc)
    nodes = got.shape[1] - BLOCK
    if part == 1:
        reps = got.shape[0]
        weight_sum[...] = sum(got[k, nodes:].astype(jnp.float32) for k in range(reps))

    def group(codes):
        products = []
        for code in codes:
            row = (code >> ROW_AT) & (ROWS - 1)
            grad = got[row // 2, pl.ds(pl.multiple_of((row % 2) * BLOCK, BLOCK), BLOCK), :]
            products.append(
                jnp.dot(grad, buffer[code & 255], preferred_element_type=jnp.float32)
            )
        for code, product in zip(codes, products):
            acc[code >> PLACE_AT] += product

    tile_groups(part, lists, group, lambda done, need: need)
    feats = own.shape[1]
    own[:SPAN] = acc[:PART].reshape(SPAN, feats)
    other[:SPAN] = acc[PART:PLACES].reshape(SPAN, feats).astype(jnp.bfloat16)
    if part == 1:
        core = lax.axis_index("core")
        mine = pl.multiple_of(core * EXTRA, EXTRA)
        theirs = pl.multiple_of((1 - core) * EXTRA, EXTRA)
        own[SPAN:] = weight_sum[pl.ds(mine, EXTRA), :]
        other[SPAN:] = weight_sum[pl.ds(theirs, EXTRA), :].astype(jnp.bfloat16)


def middle_kernel(y_parts, weight, cotangent, hidden, sent):
    reps, nodes, feats = y_parts.shape
    y = sum(y_parts[k].astype(jnp.float32) for k in range(reps))
    z = jnp.dot(
        y,
        weight[...].astype(jnp.float32),
        precision=lax.Precision.HIGHEST,
        preferred_element_type=jnp.float32,
    )
    sigma = jax.nn.sigmoid(z)
    hidden[...] = (z * sigma).astype(jnp.bfloat16)
    grad = cotangent[...].astype(jnp.float32) * sigma * (1.0 + z * (1.0 - sigma))
    weight_part = jnp.dot(
        y.T.astype(jnp.bfloat16), grad.astype(jnp.bfloat16), preferred_element_type=jnp.float32
    ).astype(jnp.bfloat16)
    for at in range(0, nodes, BLOCK):
        grad_t = grad[at : at + BLOCK].T.astype(jnp.bfloat16)
        for k in range(reps):
            sent[k, pl.ds(at, BLOCK), :] = grad_t
    for k in range(reps):
        sent[k, nodes:] = weight_part


def away_kernel(own, other, out):
    out[...] = (own[...] + other[...].astype(jnp.float32)).astype(jnp.bfloat16)


def home_kernel(own, other, away_own, away_other, came, out):
    peers = out.shape[0]
    nodes = out.shape[1] - EXTRA
    weight = away_own[SPAN:] + away_other[SPAN:].astype(jnp.float32)
    weight = (weight + came[SPAN:].astype(jnp.float32)).astype(jnp.bfloat16)
    for k in range(peers):
        here = pl.ds(k * nodes, nodes)
        total = own[here, :] + other[here, :].astype(jnp.float32)
        total = total + came[here, :].astype(jnp.float32)
        out[k, :nodes] = total.astype(jnp.bfloat16)
        out[k, nodes:] = weight


def weight_kernel(got, weight_rows):
    nodes = got.shape[1] - EXTRA
    weight_rows[...] = sum(got[k, nodes:].astype(jnp.float32) for k in range(got.shape[0]))


def feats_kernel(got, weight, grad_feats):
    nodes = grad_feats.shape[0]
    for at in range(0, nodes, BLOCK):
        here = pl.ds(at, BLOCK)
        total = sum(got[k, here].astype(jnp.float32) for k in range(got.shape[0]))
        grad_feats[here, :] = lax.dot_general(
            total.T.astype(jnp.bfloat16),
            weight[...],
            (((1,), (1,)), ((), ())),
            preferred_element_type=jnp.float32,
        ).astype(jnp.bfloat16)


def join_kernel(mine, theirs, grad_weight):
    core = lax.axis_index("core")
    at = pl.multiple_of(core * EXTRA, EXTRA)
    grad_weight[pl.ds(at, EXTRA), :] = mine[...]
    at = pl.multiple_of((1 - core) * EXTRA, EXTRA)
    grad_weight[pl.ds(at, EXTRA), :] = theirs[...]


def fan_kernel(block, out, sem):
    copy = pltpu.make_async_copy(block, out.at[0], sem)
    copy.start()
    copy.wait()
    for k in range(1, out.shape[0]):
        out[k] = out[0]


def lists_kernel(count, row_ids, col_ids, out, rows, cols, held, sems):
    moves = [
        pltpu.make_async_copy(row_ids, rows, sems.at[0]),
        pltpu.make_async_copy(col_ids, cols, sems.at[1]),
    ]
    for move in moves:
        move.start()
    for move in moves:
        move.wait()
    slots = lax.broadcasted_iota(jnp.int32, (1, CAP), 1)
    block = cols[...]
    z = (block >> 2) & 7
    core = ((block >> 1) & 1) ^ lax.axis_index("core")
    part = (z & 1) ^ lax.axis_index("zp")
    place = core * PART + ((block >> 5) * 4 + (z >> 1)) * 2 + (block & 1)
    code = slots | (rows[...] << ROW_AT) | (place << PLACE_AT)
    part = jnp.where(slots < count[0], part, 2).astype(jnp.float32)
    code = (code - SPARE).astype(jnp.float32)

    square = (CAP, CAP)
    across = jnp.broadcast_to(part, square)
    down = across.T
    code = jnp.broadcast_to(code, square).T
    lane = lax.broadcasted_iota(jnp.int32, square, 1)
    earlier = (lane < lax.broadcasted_iota(jnp.int32, square, 0)) & (across == down)
    rank = jnp.sum(jnp.where(earlier, 1.0, 0.0), axis=1, keepdims=True)
    at_rank = rank == lane.astype(jnp.float32)
    for p in range(2):
        listed = jnp.where(at_rank & (down == p), code, 0.0)
        entries = jnp.sum(listed, axis=0, keepdims=True).astype(jnp.int32) + SPARE
        size = jnp.sum(jnp.where(part == p, 1.0, 0.0), axis=1, keepdims=True)
        held[pl.ds(p, 1), :CAP] = entries
        held[pl.ds(p, 1), CAP:] = jnp.broadcast_to(size, (1, WIDTH - CAP)).astype(jnp.int32)
    copy = pltpu.make_async_copy(held, out, sems.at[2])
    copy.start()
    copy.wait()


SMEM = pl.BSMEM = pl.BSMEM = pl.BlockSpec(memory_space=pltpu.SMEM)
VMEM = pl.BlockSpec(memory_space=pltpu.VMEM)
ANY = pl.BlockSpec(memory_space=pl.ANY)


def forward_pass(part, lists, tiles, parts, before=()):
    cap = tiles.shape[0]
    out = jax.ShapeDtypeStruct(
        (ROWS, BLOCK, BLOCK), jnp.float32 if part == 0 else jnp.bfloat16
    )
    scratch = [
        pltpu.VMEM((PLACES, BLOCK, BLOCK), jnp.bfloat16),
        pltpu.VMEM((ROWS + 1, BLOCK, BLOCK), jnp.float32),
        pltpu.SemaphoreType.DMA((2,)),
    ]
    if part == 0:
        scratch.append(pltpu.SemaphoreType.DMA((cap // CHUNK,)))
    return pl.pallas_call(
        functools.partial(forward_kernel, part),
        out_shape=(out, pltpu.VMEM((cap, BLOCK, BLOCK), jnp.bfloat16)) if part == 0 else out,
        in_specs=[SMEM, ANY if part == 0 else VMEM] + [VMEM] * len(before) + [ANY, ANY],
        out_specs=(VMEM, VMEM) if part == 0 else VMEM,
        scratch_shapes=scratch,
        compiler_params=pltpu.CompilerParams(vmem_limit_bytes=20 << 20),
        cost_estimate=pl.CostEstimate(flops=1 << 30, bytes_accessed=9 << 20, transcendentals=0),
        name=f"forward_tiles_{part}",
    )(
        pltpu.with_memory_space_constraint(lists, pltpu.SMEM),
        pltpu.with_memory_space_constraint(tiles, pltpu.HBM if part == 0 else pltpu.VMEM),
        *before,
        *parts,
    )


def backward_pass(part, lists, held, got):
    feats = got.shape[2]
    size = SPAN + EXTRA * part
    scratch = [pltpu.VMEM((PLACES + 1, BLOCK, BLOCK), jnp.float32)]
    if part == 1:
        scratch.append(pltpu.VMEM((BLOCK, BLOCK), jnp.float32))
    return pl.pallas_call(
        functools.partial(backward_kernel, part),
        out_shape=(
            jax.ShapeDtypeStruct((size, feats), jnp.float32),
            jax.ShapeDtypeStruct((size, feats), jnp.bfloat16),
        ),
        in_specs=[SMEM, VMEM, VMEM],
        out_specs=(VMEM, VMEM),
        scratch_shapes=scratch,
        compiler_params=pltpu.CompilerParams(vmem_limit_bytes=20 << 20),
        cost_estimate=pl.CostEstimate(flops=1 << 30, bytes_accessed=1 << 20, transcendentals=0),
        name=f"backward_tiles_{part}",
    )(pltpu.with_memory_space_constraint(lists, pltpu.SMEM), pltpu.with_memory_space_constraint(held, pltpu.VMEM), got)


def merge(kernel, out_shape, *arrays):
    out_specs = (VMEM,) * len(out_shape) if isinstance(out_shape, tuple) else VMEM
    return pl.pallas_call(
        kernel,
        out_shape=out_shape,
        in_specs=[VMEM] * len(arrays),
        out_specs=out_specs,
        compiler_params=pltpu.CompilerParams(vmem_limit_bytes=16 << 20),
        cost_estimate=pl.CostEstimate(flops=1 << 20, bytes_accessed=4 << 20, transcendentals=0),
        name=kernel.__name__,
    )(*arrays)


def spread(block, axes):
    n = lax.axis_size(axes)
    blocks = pl.pallas_call(
        fan_kernel,
        out_shape=pltpu.VMEM((n, *block.shape), block.dtype),
        in_specs=[ANY],
        out_specs=VMEM,
        scratch_shapes=[pltpu.SemaphoreType.DMA],
        compiler_params=pltpu.CompilerParams(vmem_limit_bytes=16 << 20),
        cost_estimate=pl.CostEstimate(flops=0, bytes_accessed=1 << 16, transcendentals=0),
        name="fan",
    )(pltpu.with_memory_space_constraint(block, pltpu.HBM))
    return lax.all_to_all(blocks, axes, 0, 0)


def tile_lists(count, rows, cols):
    return pl.pallas_call(
        lists_kernel,
        out_shape=pltpu.SMEM((2, WIDTH), jnp.int32),
        in_specs=[SMEM, ANY, ANY],
        out_specs=SMEM,
        scratch_shapes=[
            pltpu.VMEM((1, CAP), jnp.int32),
            pltpu.VMEM((1, CAP), jnp.int32),
            pltpu.VMEM((2, WIDTH), jnp.int32),
            pltpu.SemaphoreType.DMA((3,)),
        ],
        compiler_params=pltpu.CompilerParams(vmem_limit_bytes=16 << 20),
        cost_estimate=pl.CostEstimate(flops=1 << 20, bytes_accessed=1 << 12, transcendentals=0),
        name="lists",
    )(
        count,
        pltpu.with_memory_space_constraint(rows, pltpu.HBM),
        pltpu.with_memory_space_constraint(cols, pltpu.HBM),
    )


def local(features, weight, cotangent, tiles, row_ids, col_ids, counts):
    x = features[0]
    nodes, feats = x.shape
    tiles = tiles[0, 0]
    lists = tile_lists(counts[0], row_ids[0], col_ids[0])
    blocks = (PART, BLOCK, feats)

    own = spread(x, PARITY)
    beside = lax.ppermute(own, ALONG, NEXT)
    own_other = lax.ppermute(own, "core", SWAP)
    y_part, held = forward_pass(
        0, lists, tiles, (own.reshape(blocks), own_other.reshape(blocks))
    )
    beside, y_part = lax.optimization_barrier((beside, y_part))
    beside_other = lax.ppermute(beside, "core", SWAP)
    y_part = forward_pass(
        1, lists, held, (beside.reshape(blocks), beside_other.reshape(blocks)), (y_part,)
    )

    reps = lax.axis_size(REP)
    y_parts = lax.all_to_all(y_part.reshape(reps, nodes, feats), REP, 0, 0)
    hidden, sent = pl.pallas_call(
        middle_kernel,
        out_shape=(
            jax.ShapeDtypeStruct((nodes, feats), jnp.bfloat16),
            pltpu.VMEM((reps, nodes + feats, feats), jnp.bfloat16),
        ),
        in_specs=[VMEM, VMEM, VMEM],
        out_specs=(VMEM, VMEM),
        compiler_params=pltpu.CompilerParams(vmem_limit_bytes=16 << 20),
        cost_estimate=pl.CostEstimate(flops=1 << 25, bytes_accessed=4 << 20, transcendentals=1 << 15),
        name="middle",
    )(y_parts, weight, cotangent[0])
    got = lax.all_to_all(sent, REP, 0, 0)
    away_own, away_other = backward_pass(1, lists, held, got)
    away_other = lax.ppermute(away_other, "core", SWAP)
    away = merge(
        away_kernel, jax.ShapeDtypeStruct(away_own.shape, jnp.bfloat16), away_own, away_other
    )
    held, away = lax.optimization_barrier((held, away))
    came = lax.ppermute(away, ALONG, NEXT)
    home_own, home_other = backward_pass(0, lists, held, got)
    home_other = lax.ppermute(home_other, "core", SWAP)
    peers = lax.axis_size(PARITY)
    sent = merge(
        home_kernel,
        pltpu.VMEM((peers, nodes + EXTRA, feats), jnp.bfloat16),
        home_own, home_other, away_own, away_other, came,
    )
    got = lax.all_to_all(sent, PARITY, 0, 0)
    mine = merge(weight_kernel, jax.ShapeDtypeStruct((EXTRA, feats), jnp.float32), got)
    theirs = lax.ppermute(mine, "core", SWAP)
    grad_feats = merge(
        feats_kernel, jax.ShapeDtypeStruct((nodes, feats), jnp.bfloat16), got, weight
    )
    grad_weight = merge(
        join_kernel, jax.ShapeDtypeStruct((feats, feats), jnp.float32), mine, theirs
    )
    return hidden[None], grad_feats.reshape(1, nodes, feats), grad_weight


def solution(mesh):
    mesh = Mesh(mesh.devices.reshape(SIZES), AXES)
    placed = P(ROW, REP)
    return jax.shard_map(
        local,
        mesh=mesh,
        in_specs=(placed, P(), placed, placed, placed, placed, placed),
        out_specs=(placed, placed, P()),
        check_vma=False,
    )
```

```python
import functools

import jax
import jax.numpy as jnp
from jax import lax
from jax.experimental import pallas as pl
from jax.experimental.pallas import tpu as pltpu
from jax.sharding import Mesh, PartitionSpec as P

CHUNK = 32
BLOCK = 128
ROWS = 16
PART = 16
CAP = 256
OWN, OWN_OTHER, BESIDE, BESIDE_OTHER = PARTS = range(4)
ROW_AT, PLACE_AT = 8, 13
SPARE = (ROWS << ROW_AT) | (PART << PLACE_AT)
COUNT_AT = CAP
WIDTH = CAP + 128
SPAN = PART * BLOCK
EXTRA = BLOCK // 2
SIZES = (4, 2, 2, 4, 2, 2)
AXES = ("x", "ylo", "yhi", "zq", "zp", "core")
REP = ("x", "ylo")
ROW = ("yhi", "zq", "zp", "core")
PARITY = ("yhi", "zq")
ALONG = ("zq", "zp", "core")
SWAP = ((0, 1), (1, 0))
NEXT = tuple((2 * z, 2 * ((z + 1) % 8)) for z in range(8)) + tuple(
    (2 * z + 1, 2 * ((z + 7) % 8) + 1) for z in range(8)
)


def tile_copy(tiles, buffer, sems, chunk):
    span = pl.ds(chunk * CHUNK, CHUNK)
    return pltpu.make_async_copy(tiles.at[span], buffer.at[span], sems.at[chunk])


def tile_groups(part, lists, group, ready=lambda done, need: need, done=0):
    count = lists[part, COUNT_AT]

    def step(k, done):
        base = k * CHUNK
        last = lists[part, jnp.minimum(base + CHUNK, count) - 1] & 255
        done = ready(done, last // CHUNK + 1)
        group([lists[part, base + u] for u in range(CHUNK)])
        return done

    return lax.fori_loop(0, (count + CHUNK - 1) // CHUNK, step, done)


def forward_group(buffer, block_ref, acc):
    def group(codes):
        products = [
            jnp.dot(
                buffer[code & 255],
                block_ref[(code >> PLACE_AT) & (PART - 1)],
                preferred_element_type=jnp.float32,
            )
            for code in codes
        ]
        for code, product in zip(codes, products):
            acc[(code >> ROW_AT) & 31] += product

    return group


def backward_group(buffer, got, acc):
    def group(codes):
        products = []
        for code in codes:
            row = (code >> ROW_AT) & (ROWS - 1)
            grad = got[row // 2, pl.ds(pl.multiple_of((row % 2) * BLOCK, BLOCK), BLOCK), :]
            products.append(
                jnp.dot(grad, buffer[code & 255], preferred_element_type=jnp.float32)
            )
        for code, product in zip(codes, products):
            acc[code >> PLACE_AT] += product

    return group


def first_forward_kernel(lists, tiles, x0, x1, out, buffer, acc, sems):
    chunks = (sum(lists[part, COUNT_AT] for part in PARTS) + CHUNK - 1) // CHUNK

    @pl.loop(0, chunks)
    def _(c):
        tile_copy(tiles, buffer, sems, c).start()

    acc[...] = jnp.zeros_like(acc)

    def ready(done, need):
        @pl.loop(done, need)
        def _(c):
            tile_copy(tiles, buffer, sems, c).wait()

        return jnp.maximum(done, need)

    done = tile_groups(OWN, lists, forward_group(buffer, x0, acc), ready, 0)
    done = tile_groups(OWN_OTHER, lists, forward_group(buffer, x1, acc), ready, done)
    ready(done, chunks)
    out[...] = acc[:ROWS]


def forward_kernel(part, lists, buffer, before, x, out, acc):
    acc[:ROWS] = before[...]
    tile_groups(part, lists, forward_group(buffer, x, acc))
    out[...] = acc[:ROWS].astype(out.dtype)


def away_part_kernel(part, lists, buffer, got, out, acc, weight_sum):
    acc[...] = jnp.zeros_like(acc)
    nodes = got.shape[1] - BLOCK
    weight_sum[...] = sum(got[k, nodes:].astype(jnp.float32) for k in range(got.shape[0]))
    tile_groups(part, lists, backward_group(buffer, got, acc))
    out[:SPAN] = acc[:PART].reshape(SPAN, out.shape[1]).astype(out.dtype)
    core = lax.axis_index("core")
    at = pl.multiple_of((core if part == BESIDE else 1 - core) * EXTRA, EXTRA)
    out[SPAN:] = weight_sum[pl.ds(at, EXTRA), :].astype(out.dtype)


def home_part_kernel(lists, buffer, got, own, other, acc, acc_other):
    for part, out, sums in ((OWN_OTHER, other, acc_other), (OWN, own, acc)):
        sums[...] = jnp.zeros_like(sums)
        tile_groups(part, lists, backward_group(buffer, got, sums))
        out[...] = sums[:PART].reshape(out.shape).astype(out.dtype)


def middle_kernel(y_parts, weight, cotangent, hidden, sent):
    reps, nodes, feats = y_parts.shape
    y = sum(y_parts[k].astype(jnp.float32) for k in range(reps))
    z = jnp.dot(
        y,
        weight[...].astype(jnp.float32),
        precision=lax.Precision.HIGHEST,
        preferred_element_type=jnp.float32,
    )
    sigma = jax.nn.sigmoid(z)
    hidden[...] = (z * sigma).astype(jnp.bfloat16)
    grad = cotangent[...].astype(jnp.float32) * sigma * (1.0 + z * (1.0 - sigma))
    weight_part = jnp.dot(
        y.T.astype(jnp.bfloat16), grad.astype(jnp.bfloat16), preferred_element_type=jnp.float32
    ).astype(jnp.bfloat16)
    for at in range(0, nodes, BLOCK):
        grad_t = grad[at : at + BLOCK].T.astype(jnp.bfloat16)
        for k in range(reps):
            sent[k, pl.ds(at, BLOCK), :] = grad_t
    for k in range(reps):
        sent[k, nodes:] = weight_part


def away_kernel(own, other, out):
    out[...] = (own[...] + other[...].astype(jnp.float32)).astype(jnp.bfloat16)


def home_kernel(own, other, away_own, away_other, came, out):
    peers = out.shape[0]
    nodes = out.shape[1] - EXTRA
    weight = away_own[SPAN:] + away_other[SPAN:].astype(jnp.float32)
    weight = (weight + came[SPAN:].astype(jnp.float32)).astype(jnp.bfloat16)
    for k in range(peers):
        here = pl.ds(k * nodes, nodes)
        total = own[here, :] + other[here, :].astype(jnp.float32)
        total = total + came[here, :].astype(jnp.float32)
        out[k, :nodes] = total.astype(jnp.bfloat16)
        out[k, nodes:] = weight


def weight_kernel(got, weight_rows):
    nodes = got.shape[1] - EXTRA
    weight_rows[...] = sum(got[k, nodes:].astype(jnp.float32) for k in range(got.shape[0]))


def feats_kernel(got, weight, grad_feats):
    nodes = grad_feats.shape[0]
    for at in range(0, nodes, BLOCK):
        here = pl.ds(at, BLOCK)
        total = sum(got[k, here].astype(jnp.float32) for k in range(got.shape[0]))
        grad_feats[here, :] = lax.dot_general(
            total.T.astype(jnp.bfloat16),
            weight[...],
            (((1,), (1,)), ((), ())),
            preferred_element_type=jnp.float32,
        ).astype(jnp.bfloat16)


def join_kernel(mine, theirs, grad_weight):
    core = lax.axis_index("core")
    at = pl.multiple_of(core * EXTRA, EXTRA)
    grad_weight[pl.ds(at, EXTRA), :] = mine[...]
    at = pl.multiple_of((1 - core) * EXTRA, EXTRA)
    grad_weight[pl.ds(at, EXTRA), :] = theirs[...]


def fan_kernel(block, out, sem):
    copy = pltpu.make_async_copy(block, out.at[0], sem)
    copy.start()
    copy.wait()
    for k in range(1, out.shape[0]):
        out[k] = out[0]


def lists_kernel(count, row_ids, col_ids, out, rows, cols, held, sems):
    moves = [
        pltpu.make_async_copy(row_ids, rows, sems.at[0]),
        pltpu.make_async_copy(col_ids, cols, sems.at[1]),
    ]
    for move in moves:
        move.start()
    for move in moves:
        move.wait()
    slots = lax.broadcasted_iota(jnp.int32, (1, CAP), 1)
    block = cols[...]
    z = (block >> 2) & 7
    core = ((block >> 1) & 1) ^ lax.axis_index("core")
    part = ((z & 1) ^ lax.axis_index("zp")) * 2 + core
    place = ((block >> 5) * 4 + (z >> 1)) * 2 + (block & 1)
    code = slots | (rows[...] << ROW_AT) | (place << PLACE_AT)
    part = jnp.where(slots < count[0], part, len(PARTS)).astype(jnp.float32)
    code = (code - SPARE).astype(jnp.float32)

    square = (CAP, CAP)
    across = jnp.broadcast_to(part, square)
    down = across.T
    code = jnp.broadcast_to(code, square).T
    lane = lax.broadcasted_iota(jnp.int32, square, 1)
    earlier = (lane < lax.broadcasted_iota(jnp.int32, square, 0)) & (across == down)
    rank = jnp.sum(jnp.where(earlier, 1.0, 0.0), axis=1, keepdims=True)
    at_rank = rank == lane.astype(jnp.float32)
    for p in PARTS:
        listed = jnp.where(at_rank & (down == p), code, 0.0)
        entries = jnp.sum(listed, axis=0, keepdims=True).astype(jnp.int32) + SPARE
        size = jnp.sum(jnp.where(part == p, 1.0, 0.0), axis=1, keepdims=True)
        held[pl.ds(p, 1), :CAP] = entries
        held[pl.ds(p, 1), CAP:] = jnp.broadcast_to(size, (1, WIDTH - CAP)).astype(jnp.int32)
    copy = pltpu.make_async_copy(held, out, sems.at[2])
    copy.start()
    copy.wait()


SMEM = pl.BSMEM = pl.BSMEM = pl.BlockSpec(memory_space=pltpu.SMEM)
VMEM = pl.BlockSpec(memory_space=pltpu.VMEM)
ANY = pl.BlockSpec(memory_space=pl.ANY)


def tile_kernel(kernel, out_shape, lists, tiles, arrays, scratch):
    first = kernel is first_forward_kernel
    out_specs = (VMEM,) * len(out_shape) if isinstance(out_shape, tuple) else VMEM
    return pl.pallas_call(
        kernel,
        out_shape=out_shape,
        in_specs=[SMEM, ANY if first else VMEM] + [VMEM] * len(arrays),
        out_specs=out_specs,
        scratch_shapes=scratch,
        compiler_params=pltpu.CompilerParams(vmem_limit_bytes=16 << 20),
        cost_estimate=pl.CostEstimate(flops=1 << 29, bytes_accessed=4 << 20, transcendentals=0),
        name=getattr(kernel, "func", kernel).__name__,
    )(
        pltpu.with_memory_space_constraint(lists, pltpu.SMEM),
        pltpu.with_memory_space_constraint(tiles, pltpu.HBM if first else pltpu.VMEM),
        *arrays,
    )


def sums(rows):
    return pltpu.VMEM((rows + 1, BLOCK, BLOCK), jnp.float32)


def merge(kernel, out_shape, *arrays):
    out_specs = (VMEM,) * len(out_shape) if isinstance(out_shape, tuple) else VMEM
    return pl.pallas_call(
        kernel,
        out_shape=out_shape,
        in_specs=[VMEM] * len(arrays),
        out_specs=out_specs,
        compiler_params=pltpu.CompilerParams(vmem_limit_bytes=16 << 20),
        cost_estimate=pl.CostEstimate(flops=1 << 20, bytes_accessed=4 << 20, transcendentals=0),
        name=kernel.__name__,
    )(*arrays)


def spread(block, axes):
    n = lax.axis_size(axes)
    blocks = pl.pallas_call(
        fan_kernel,
        out_shape=pltpu.VMEM((n, *block.shape), block.dtype),
        in_specs=[ANY],
        out_specs=VMEM,
        scratch_shapes=[pltpu.SemaphoreType.DMA],
        compiler_params=pltpu.CompilerParams(vmem_limit_bytes=16 << 20),
        cost_estimate=pl.CostEstimate(flops=0, bytes_accessed=1 << 16, transcendentals=0),
        name="fan",
    )(pltpu.with_memory_space_constraint(block, pltpu.HBM))
    return lax.all_to_all(blocks, axes, 0, 0)


def tile_lists(count, rows, cols):
    return pl.pallas_call(
        lists_kernel,
        out_shape=pltpu.SMEM((len(PARTS), WIDTH), jnp.int32),
        in_specs=[SMEM, ANY, ANY],
        out_specs=SMEM,
        scratch_shapes=[
            pltpu.VMEM((1, CAP), jnp.int32),
            pltpu.VMEM((1, CAP), jnp.int32),
            pltpu.VMEM((len(PARTS), WIDTH), jnp.int32),
            pltpu.SemaphoreType.DMA((3,)),
        ],
        compiler_params=pltpu.CompilerParams(vmem_limit_bytes=16 << 20),
        cost_estimate=pl.CostEstimate(flops=1 << 20, bytes_accessed=1 << 12, transcendentals=0),
        name="lists",
    )(
        count,
        pltpu.with_memory_space_constraint(rows, pltpu.HBM),
        pltpu.with_memory_space_constraint(cols, pltpu.HBM),
    )


def local(features, weight, cotangent, tiles, row_ids, col_ids, counts):
    x = features[0]
    nodes, feats = x.shape
    tiles = tiles[0, 0]
    blocks = (PART, BLOCK, feats)
    own = spread(x, PARITY)
    beside = lax.ppermute(own, ALONG, NEXT)
    lists = tile_lists(counts[0], row_ids[0], col_ids[0])
    own_other = lax.ppermute(own, "core", SWAP)
    y_shape = jax.ShapeDtypeStruct((ROWS, BLOCK, BLOCK), jnp.float32)
    y_part, held = tile_kernel(
        first_forward_kernel,
        (y_shape, pltpu.VMEM(tiles.shape, jnp.bfloat16)),
        lists,
        tiles,
        (own.reshape(blocks), own_other.reshape(blocks)),
        [sums(ROWS), pltpu.SemaphoreType.DMA((CAP // CHUNK,))],
    )
    beside, y_part = lax.optimization_barrier((beside, y_part))
    beside_other = lax.ppermute(beside, "core", SWAP)
    y_part = tile_kernel(
        functools.partial(forward_kernel, BESIDE),
        y_shape, lists, held, (y_part, beside.reshape(blocks)), [sums(ROWS)],
    )
    y_part = tile_kernel(
        functools.partial(forward_kernel, BESIDE_OTHER),
        jax.ShapeDtypeStruct((ROWS, BLOCK, BLOCK), jnp.bfloat16),
        lists, held, (y_part, beside_other.reshape(blocks)), [sums(ROWS)],
    )

    reps = lax.axis_size(REP)
    y_parts = lax.all_to_all(y_part.reshape(reps, nodes, feats), REP, 0, 0)
    hidden, sent = pl.pallas_call(
        middle_kernel,
        out_shape=(
            jax.ShapeDtypeStruct((nodes, feats), jnp.bfloat16),
            pltpu.VMEM((reps, nodes + feats, feats), jnp.bfloat16),
        ),
        in_specs=[VMEM, VMEM, VMEM],
        out_specs=(VMEM, VMEM),
        compiler_params=pltpu.CompilerParams(vmem_limit_bytes=16 << 20),
        cost_estimate=pl.CostEstimate(flops=1 << 25, bytes_accessed=4 << 20, transcendentals=1 << 15),
        name="middle",
    )(y_parts, weight, cotangent[0])
    got = lax.all_to_all(sent, REP, 0, 0)
    def away_part(part, dtype):
        return tile_kernel(
            functools.partial(away_part_kernel, part),
            jax.ShapeDtypeStruct((SPAN + EXTRA, feats), dtype),
            lists, held, (got,), [sums(PART), pltpu.VMEM((BLOCK, feats), jnp.float32)],
        )

    away_other = lax.ppermute(away_part(BESIDE_OTHER, jnp.bfloat16), "core", SWAP)
    away_own = away_part(BESIDE, jnp.float32)
    away = merge(
        away_kernel, jax.ShapeDtypeStruct(away_own.shape, jnp.bfloat16), away_own, away_other
    )
    held, away = lax.optimization_barrier((held, away))
    came = lax.ppermute(away, ALONG, NEXT)
    home_own, home_other = tile_kernel(
        home_part_kernel,
        (
            jax.ShapeDtypeStruct((SPAN, feats), jnp.float32),
            jax.ShapeDtypeStruct((SPAN, feats), jnp.bfloat16),
        ),
        lists, held, (got,), [sums(PART), sums(PART)],
    )
    home_other = lax.ppermute(home_other, "core", SWAP)
    peers = lax.axis_size(PARITY)
    sent = merge(
        home_kernel,
        pltpu.VMEM((peers, nodes + EXTRA, feats), jnp.bfloat16),
        home_own, home_other, away_own, away_other, came,
    )
    got = lax.all_to_all(sent, PARITY, 0, 0)
    mine = merge(weight_kernel, jax.ShapeDtypeStruct((EXTRA, feats), jnp.float32), got)
    theirs = lax.ppermute(mine, "core", SWAP)
    grad_feats = merge(
        feats_kernel, jax.ShapeDtypeStruct((nodes, feats), jnp.bfloat16), got, weight
    )
    grad_weight = merge(
        join_kernel, jax.ShapeDtypeStruct((feats, feats), jnp.float32), mine, theirs
    )
    return hidden[None], grad_feats.reshape(1, nodes, feats), grad_weight


def solution(mesh):
    mesh = Mesh(mesh.devices.reshape(SIZES), AXES)
    placed = P(ROW, REP)
    return jax.shard_map(
        local,
        mesh=mesh,
        in_specs=(placed, P(), placed, placed, placed, placed, placed),
        out_specs=(placed, placed, P()),
        check_vma=False,
    )
```

```python
import functools

import jax
import jax.numpy as jnp
from jax import lax
from jax.experimental import pallas as pl
from jax.experimental.pallas import tpu as pltpu
from jax.sharding import Mesh, PartitionSpec as P

CHUNK = 32
BLOCK = 128
ROWS = 16
PART = 16
CAP = 256
OWN, OWN_OTHER, BESIDE, BESIDE_OTHER = PARTS = range(4)
ROW_AT, PLACE_AT = 8, 13
SPARE = (ROWS << ROW_AT) | (PART << PLACE_AT)
COUNT_AT = CAP
WIDTH = CAP + 128
SPAN = PART * BLOCK
EXTRA = BLOCK // 2
SIZES = (4, 2, 2, 4, 2, 2)
AXES = ("x", "ylo", "yhi", "zq", "zp", "core")
REP = ("x", "ylo")
ROW = ("yhi", "zq", "zp", "core")
PARITY = ("yhi", "zq")
ALONG = ("zq", "zp", "core")
SWAP = ((0, 1), (1, 0))
NEXT = tuple((2 * z, 2 * ((z + 1) % 8)) for z in range(8)) + tuple(
    (2 * z + 1, 2 * ((z + 7) % 8) + 1) for z in range(8)
)


def tile_copy(tiles, buffer, sems, chunk):
    span = pl.ds(chunk * CHUNK, CHUNK)
    return pltpu.make_async_copy(tiles.at[span], buffer.at[span], sems.at[chunk])


def tile_groups(part, lists, group):
    @pl.loop(0, (lists[part, COUNT_AT] + CHUNK - 1) // CHUNK)
    def _(k):
        group([lists[part, k * CHUNK + u] for u in range(CHUNK)])


def forward_group(buffer, block_ref, acc):
    def group(codes):
        products = [
            jnp.dot(
                buffer[code & 255],
                block_ref[(code >> PLACE_AT) & (PART - 1)],
                preferred_element_type=jnp.float32,
            )
            for code in codes
        ]
        for code, product in zip(codes, products):
            acc[(code >> ROW_AT) & 31] += product

    return group


def backward_group(buffer, got, acc):
    def group(codes):
        products = []
        for code in codes:
            row = (code >> ROW_AT) & (ROWS - 1)
            grad = got[row // 2, pl.ds(pl.multiple_of((row % 2) * BLOCK, BLOCK), BLOCK), :]
            products.append(
                jnp.dot(grad, buffer[code & 255], preferred_element_type=jnp.float32)
            )
        for code, product in zip(codes, products):
            acc[code >> PLACE_AT] += product

    return group


def make_lists(count, row_ids, col_ids, out, rows, cols, held, sems):
    moves = [
        pltpu.make_async_copy(row_ids, rows, sems.at[0]),
        pltpu.make_async_copy(col_ids, cols, sems.at[1]),
    ]
    for move in moves:
        move.start()
    for move in moves:
        move.wait()
    slots = lax.broadcasted_iota(jnp.int32, (1, CAP), 1)
    block = cols[...]
    z = (block >> 2) & 7
    core = ((block >> 1) & 1) ^ lax.axis_index("core")
    part = ((z & 1) ^ lax.axis_index("zp")) * 2 + core
    place = ((block >> 5) * 4 + (z >> 1)) * 2 + (block & 1)
    code = slots | (rows[...] << ROW_AT) | (place << PLACE_AT)
    part = jnp.where(slots < count[0], part, len(PARTS)).astype(jnp.float32)
    code = (code - SPARE).astype(jnp.float32)

    square = (CAP, CAP)
    across = jnp.broadcast_to(part, square)
    down = across.T
    code = jnp.broadcast_to(code, square).T
    lane = lax.broadcasted_iota(jnp.int32, square, 1)
    earlier = (lane < lax.broadcasted_iota(jnp.int32, square, 0)) & (across == down)
    rank = jnp.sum(jnp.where(earlier, 1.0, 0.0), axis=1, keepdims=True)
    at_rank = rank == lane.astype(jnp.float32)
    for p in PARTS:
        listed = jnp.where(at_rank & (down == p), code, 0.0)
        entries = jnp.sum(listed, axis=0, keepdims=True).astype(jnp.int32) + SPARE
        size = jnp.sum(jnp.where(part == p, 1.0, 0.0), axis=1, keepdims=True)
        held[pl.ds(p, 1), :CAP] = entries
        held[pl.ds(p, 1), CAP:] = jnp.broadcast_to(size, (1, WIDTH - CAP)).astype(jnp.int32)
    copy = pltpu.make_async_copy(held, out, sems.at[2])
    copy.start()
    copy.wait()


def first_forward_kernel(
    count, row_ids, col_ids, tiles, x0, x1, out, buffer, lists, acc, rows, cols, held, sems, ids_sems
):
    chunks = (count[0] + CHUNK - 1) // CHUNK

    @pl.loop(0, chunks)
    def _(c):
        tile_copy(tiles, buffer, sems, c).start()

    make_lists(count, row_ids, col_ids, lists, rows, cols, held, ids_sems)
    acc[...] = jnp.zeros_like(acc)

    def ready(done, need):
        @pl.loop(done, need)
        def _(c):
            tile_copy(tiles, buffer, sems, c).wait()

        return jnp.maximum(done, need)

    works = ((OWN, forward_group(buffer, x0, acc)), (OWN_OTHER, forward_group(buffer, x1, acc)))
    counts = [lists[part, COUNT_AT] for part, _ in works]

    def step(k, done):
        base = k * CHUNK
        for (part, group), size in zip(works, counts):
            last = lists[part, jnp.maximum(jnp.minimum(base + CHUNK, size) - 1, 0)] & 255
            done = ready(done, jnp.where(base < size, last // CHUNK + 1, done))

            @pl.when(base < size)
            def _():
                group([lists[part, base + u] for u in range(CHUNK)])

        return done

    done = lax.fori_loop(0, (jnp.maximum(*counts) + CHUNK - 1) // CHUNK, step, 0)
    ready(done, chunks)
    out[...] = acc[:ROWS]


def forward_kernel(part, lists, buffer, before, x, out, acc):
    acc[:ROWS] = before[...]
    tile_groups(part, lists, forward_group(buffer, x, acc))
    out[...] = acc[:ROWS].astype(out.dtype)


def away_part_kernel(part, lists, buffer, got, out, acc, weight_sum):
    acc[...] = jnp.zeros_like(acc)
    nodes = got.shape[1] - BLOCK
    weight_sum[...] = sum(got[k, nodes:].astype(jnp.float32) for k in range(got.shape[0]))
    tile_groups(part, lists, backward_group(buffer, got, acc))
    out[:SPAN] = acc[:PART].reshape(SPAN, out.shape[1]).astype(out.dtype)
    core = lax.axis_index("core")
    at = pl.multiple_of((core if part == BESIDE else 1 - core) * EXTRA, EXTRA)
    out[SPAN:] = weight_sum[pl.ds(at, EXTRA), :].astype(out.dtype)


def home_part_kernel(lists, buffer, got, own, other, acc, acc_other):
    for part, out, sums in ((OWN_OTHER, other, acc_other), (OWN, own, acc)):
        sums[...] = jnp.zeros_like(sums)
        tile_groups(part, lists, backward_group(buffer, got, sums))
        out[...] = sums[:PART].reshape(out.shape).astype(out.dtype)


def middle_kernel(y_parts, weight, cotangent, z_out, sent):
    reps, nodes, feats = y_parts.shape
    y = sum(y_parts[k].astype(jnp.float32) for k in range(reps))
    z = jnp.dot(
        y,
        weight[...].astype(jnp.float32),
        precision=lax.Precision.HIGHEST,
        preferred_element_type=jnp.float32,
    )
    sigma = jax.nn.sigmoid(z)
    z_out[...] = z
    grad = cotangent[...].astype(jnp.float32) * sigma * (1.0 + z * (1.0 - sigma))
    weight_part = jnp.dot(
        y.T.astype(jnp.bfloat16), grad.astype(jnp.bfloat16), preferred_element_type=jnp.float32
    ).astype(jnp.bfloat16)
    for at in range(0, nodes, BLOCK):
        grad_t = grad[at : at + BLOCK].T.astype(jnp.bfloat16)
        for k in range(reps):
            sent[k, pl.ds(at, BLOCK), :] = grad_t
    for k in range(reps):
        sent[k, nodes:] = weight_part


def hidden_kernel(z, hidden):
    hidden[...] = (z[...] * jax.nn.sigmoid(z[...])).astype(jnp.bfloat16)


def away_kernel(own, other, out):
    out[...] = (own[...] + other[...].astype(jnp.float32)).astype(jnp.bfloat16)


def home_kernel(own, other, away_own, away_other, came, out):
    peers = out.shape[0]
    nodes = out.shape[1] - EXTRA
    weight = away_own[SPAN:] + away_other[SPAN:].astype(jnp.float32)
    weight = (weight + came[SPAN:].astype(jnp.float32)).astype(jnp.bfloat16)
    for k in range(peers):
        here = pl.ds(k * nodes, nodes)
        total = own[here, :] + other[here, :].astype(jnp.float32)
        total = total + came[here, :].astype(jnp.float32)
        out[k, :nodes] = total.astype(jnp.bfloat16)
        out[k, nodes:] = weight


def weight_kernel(got, weight_rows):
    nodes = got.shape[1] - EXTRA
    weight_rows[...] = sum(got[k, nodes:].astype(jnp.float32) for k in range(got.shape[0]))


def feats_kernel(got, weight, grad_feats):
    nodes = grad_feats.shape[0]
    for at in range(0, nodes, BLOCK):
        here = pl.ds(at, BLOCK)
        total = sum(got[k, here].astype(jnp.float32) for k in range(got.shape[0]))
        grad_feats[here, :] = lax.dot_general(
            total.T.astype(jnp.bfloat16),
            weight[...],
            (((1,), (1,)), ((), ())),
            preferred_element_type=jnp.float32,
        ).astype(jnp.bfloat16)


def join_kernel(mine, theirs, grad_weight):
    core = lax.axis_index("core")
    at = pl.multiple_of(core * EXTRA, EXTRA)
    grad_weight[pl.ds(at, EXTRA), :] = mine[...]
    at = pl.multiple_of((1 - core) * EXTRA, EXTRA)
    grad_weight[pl.ds(at, EXTRA), :] = theirs[...]


def fan_kernel(block, out, sem):
    copy = pltpu.make_async_copy(block, out.at[0], sem)
    copy.start()
    copy.wait()
    for k in range(1, out.shape[0]):
        out[k] = out[0]


SMEM = pl.BSMEM = pl.BSMEM = pl.BlockSpec(memory_space=pltpu.SMEM)
VMEM = pl.BlockSpec(memory_space=pltpu.VMEM)
ANY = pl.BlockSpec(memory_space=pl.ANY)


def tile_kernel(kernel, out_shape, lists, held, arrays, scratch):
    out_specs = (VMEM,) * len(out_shape) if isinstance(out_shape, tuple) else VMEM
    return pl.pallas_call(
        kernel,
        out_shape=out_shape,
        in_specs=[SMEM, VMEM] + [VMEM] * len(arrays),
        out_specs=out_specs,
        scratch_shapes=scratch,
        compiler_params=pltpu.CompilerParams(vmem_limit_bytes=16 << 20),
        cost_estimate=pl.CostEstimate(flops=1 << 29, bytes_accessed=4 << 20, transcendentals=0),
        name=getattr(kernel, "func", kernel).__name__,
    )(
        pltpu.with_memory_space_constraint(lists, pltpu.SMEM),
        pltpu.with_memory_space_constraint(held, pltpu.VMEM),
        *arrays,
    )


def sums(rows):
    return pltpu.VMEM((rows + 1, BLOCK, BLOCK), jnp.float32)


def merge(kernel, out_shape, *arrays):
    out_specs = (VMEM,) * len(out_shape) if isinstance(out_shape, tuple) else VMEM
    return pl.pallas_call(
        kernel,
        out_shape=out_shape,
        in_specs=[VMEM] * len(arrays),
        out_specs=out_specs,
        compiler_params=pltpu.CompilerParams(vmem_limit_bytes=16 << 20),
        cost_estimate=pl.CostEstimate(flops=1 << 20, bytes_accessed=4 << 20, transcendentals=0),
        name=kernel.__name__,
    )(*arrays)


def spread(block, axes):
    n = lax.axis_size(axes)
    blocks = pl.pallas_call(
        fan_kernel,
        out_shape=pltpu.VMEM((n, *block.shape), block.dtype),
        in_specs=[ANY],
        out_specs=VMEM,
        scratch_shapes=[pltpu.SemaphoreType.DMA],
        compiler_params=pltpu.CompilerParams(vmem_limit_bytes=16 << 20),
        cost_estimate=pl.CostEstimate(flops=0, bytes_accessed=1 << 16, transcendentals=0),
        name="fan",
    )(pltpu.with_memory_space_constraint(block, pltpu.HBM))
    return lax.all_to_all(blocks, axes, 0, 0)


def local(features, weight, cotangent, tiles, row_ids, col_ids, counts):
    x = features[0]
    nodes, feats = x.shape
    tiles = tiles[0, 0]
    blocks = (PART, BLOCK, feats)
    own = spread(x, PARITY)
    beside = lax.ppermute(own, ALONG, NEXT)
    own_other = lax.ppermute(own, "core", SWAP)
    y_shape = jax.ShapeDtypeStruct((ROWS, BLOCK, BLOCK), jnp.float32)
    y_part, held, lists = pl.pallas_call(
        first_forward_kernel,
        out_shape=(
            y_shape,
            pltpu.VMEM(tiles.shape, jnp.bfloat16),
            pltpu.SMEM((len(PARTS), WIDTH), jnp.int32),
        ),
        in_specs=[SMEM, ANY, ANY, ANY, VMEM, VMEM],
        out_specs=(VMEM, VMEM, SMEM),
        scratch_shapes=[
            sums(ROWS),
            pltpu.VMEM((1, CAP), jnp.int32),
            pltpu.VMEM((1, CAP), jnp.int32),
            pltpu.VMEM((len(PARTS), WIDTH), jnp.int32),
            pltpu.SemaphoreType.DMA((CAP // CHUNK,)),
            pltpu.SemaphoreType.DMA((3,)),
        ],
        compiler_params=pltpu.CompilerParams(vmem_limit_bytes=16 << 20),
        cost_estimate=pl.CostEstimate(flops=1 << 30, bytes_accessed=9 << 20, transcendentals=0),
        name="first_forward",
    )(
        counts[0],
        *[pltpu.with_memory_space_constraint(a, pltpu.HBM) for a in (row_ids[0], col_ids[0], tiles)],
        own.reshape(blocks),
        own_other.reshape(blocks),
    )
    beside, y_part = lax.optimization_barrier((beside, y_part))
    beside_other = lax.ppermute(beside, "core", SWAP)
    y_part = tile_kernel(
        functools.partial(forward_kernel, BESIDE),
        y_shape, lists, held, (y_part, beside.reshape(blocks)), [sums(ROWS)],
    )
    y_part = tile_kernel(
        functools.partial(forward_kernel, BESIDE_OTHER),
        jax.ShapeDtypeStruct((ROWS, BLOCK, BLOCK), jnp.bfloat16),
        lists, held, (y_part, beside_other.reshape(blocks)), [sums(ROWS)],
    )

    reps = lax.axis_size(REP)
    y_parts = lax.all_to_all(y_part.reshape(reps, nodes, feats), REP, 0, 0)
    z, sent = pl.pallas_call(
        middle_kernel,
        out_shape=(
            jax.ShapeDtypeStruct((nodes, feats), jnp.float32),
            pltpu.VMEM((reps, nodes + feats, feats), jnp.bfloat16),
        ),
        in_specs=[VMEM, VMEM, VMEM],
        out_specs=(VMEM, VMEM),
        compiler_params=pltpu.CompilerParams(vmem_limit_bytes=16 << 20),
        cost_estimate=pl.CostEstimate(flops=1 << 25, bytes_accessed=4 << 20, transcendentals=1 << 15),
        name="middle",
    )(y_parts, weight, cotangent[0])
    got = lax.all_to_all(sent, REP, 0, 0)
    def away_part(part, dtype):
        return tile_kernel(
            functools.partial(away_part_kernel, part),
            jax.ShapeDtypeStruct((SPAN + EXTRA, feats), dtype),
            lists, held, (got,), [sums(PART), pltpu.VMEM((BLOCK, feats), jnp.float32)],
        )

    away_other = lax.ppermute(away_part(BESIDE_OTHER, jnp.bfloat16), "core", SWAP)
    away_own = away_part(BESIDE, jnp.float32)
    away = merge(
        away_kernel, jax.ShapeDtypeStruct(away_own.shape, jnp.bfloat16), away_own, away_other
    )
    held, z, away = lax.optimization_barrier((held, z, away))
    came = lax.ppermute(away, ALONG, NEXT)
    home_own, home_other = tile_kernel(
        home_part_kernel,
        (
            jax.ShapeDtypeStruct((SPAN, feats), jnp.float32),
            jax.ShapeDtypeStruct((SPAN, feats), jnp.bfloat16),
        ),
        lists, held, (got,), [sums(PART), sums(PART)],
    )
    hidden = merge(hidden_kernel, jax.ShapeDtypeStruct((nodes, feats), jnp.bfloat16), z)
    home_other, hidden = lax.optimization_barrier((home_other, hidden))
    home_other = lax.ppermute(home_other, "core", SWAP)
    peers = lax.axis_size(PARITY)
    sent = merge(
        home_kernel,
        pltpu.VMEM((peers, nodes + EXTRA, feats), jnp.bfloat16),
        home_own, home_other, away_own, away_other, came,
    )
    got = lax.all_to_all(sent, PARITY, 0, 0)
    mine = merge(weight_kernel, jax.ShapeDtypeStruct((EXTRA, feats), jnp.float32), got)
    theirs = lax.ppermute(mine, "core", SWAP)
    grad_feats = merge(
        feats_kernel, jax.ShapeDtypeStruct((nodes, feats), jnp.bfloat16), got, weight
    )
    grad_weight = merge(
        join_kernel, jax.ShapeDtypeStruct((feats, feats), jnp.float32), mine, theirs
    )
    return hidden[None], grad_feats.reshape(1, nodes, feats), grad_weight


def solution(mesh):
    mesh = Mesh(mesh.devices.reshape(SIZES), AXES)
    placed = P(ROW, REP)
    return jax.shard_map(
        local,
        mesh=mesh,
        in_specs=(placed, P(), placed, placed, placed, placed, placed),
        out_specs=(placed, placed, P()),
        check_vma=False,
    )
```

```python
import functools

import jax
import jax.numpy as jnp
from jax import lax
from jax.experimental import pallas as pl
from jax.experimental.pallas import tpu as pltpu
from jax.sharding import Mesh, PartitionSpec as P

CHUNK = 32
BLOCK = 128
ROWS = 16
PART = 16
CAP = 256
OWN, OWN_OTHER, BESIDE, BESIDE_OTHER = PARTS = range(4)
ROW_AT, PLACE_AT = 8, 13
SPARE = (ROWS << ROW_AT) | (PART << PLACE_AT)
COUNT_AT = CAP
WIDTH = CAP + 128
SPAN = PART * BLOCK
EXTRA = BLOCK // 4
SIZES = (4, 2, 2, 4, 2, 2)
AXES = ("x", "ylo", "yhi", "zq", "zp", "core")
REP = ("x", "ylo")
ROW = ("yhi", "zq", "zp", "core")
PARITY = ("yhi", "zq")
ALONG = ("zq", "zp", "core")
SWAP = ((0, 1), (1, 0))
NEXT = tuple((2 * z, 2 * ((z + 1) % 8)) for z in range(8)) + tuple(
    (2 * z + 1, 2 * ((z + 7) % 8) + 1) for z in range(8)
)


def tile_copy(tiles, buffer, sems, chunk):
    span = pl.ds(chunk * CHUNK, CHUNK)
    return pltpu.make_async_copy(tiles.at[span], buffer.at[span], sems.at[chunk])


def tile_groups(part, lists, group):
    @pl.loop(0, (lists[part, COUNT_AT] + CHUNK - 1) // CHUNK)
    def _(k):
        group([lists[part, k * CHUNK + u] for u in range(CHUNK)])


def forward_group(buffer, block_ref, acc):
    def group(codes):
        products = [
            jnp.dot(
                buffer[code & 255],
                block_ref[(code >> PLACE_AT) & (PART - 1)],
                preferred_element_type=jnp.float32,
            )
            for code in codes
        ]
        for code, product in zip(codes, products):
            acc[(code >> ROW_AT) & 31] += product

    return group


def backward_group(buffer, got, acc):
    def group(codes):
        products = []
        for code in codes:
            row = (code >> ROW_AT) & (ROWS - 1)
            grad = got[row // 2, pl.ds(pl.multiple_of((row % 2) * BLOCK, BLOCK), BLOCK), :]
            products.append(
                jnp.dot(grad, buffer[code & 255], preferred_element_type=jnp.float32)
            )
        for code, product in zip(codes, products):
            acc[code >> PLACE_AT] += product

    return group


def make_lists(count, row_ids, col_ids, out, rows, cols, held, sems):
    moves = [
        pltpu.make_async_copy(row_ids, rows, sems.at[0]),
        pltpu.make_async_copy(col_ids, cols, sems.at[1]),
    ]
    for move in moves:
        move.start()
    for move in moves:
        move.wait()
    slots = lax.broadcasted_iota(jnp.int32, (1, CAP), 1)
    block = cols[...]
    z = (block >> 2) & 7
    core = ((block >> 1) & 1) ^ lax.axis_index("core")
    part = ((z & 1) ^ lax.axis_index("zp")) * 2 + core
    place = ((block >> 5) * 4 + (z >> 1)) * 2 + (block & 1)
    code = slots | (rows[...] << ROW_AT) | (place << PLACE_AT)
    part = jnp.where(slots < count[0], part, len(PARTS)).astype(jnp.float32)
    code = (code - SPARE).astype(jnp.float32)

    square = (CAP, CAP)
    across = jnp.broadcast_to(part, square)
    down = across.T
    code = jnp.broadcast_to(code, square).T
    lane = lax.broadcasted_iota(jnp.int32, square, 1)
    earlier = (lane < lax.broadcasted_iota(jnp.int32, square, 0)) & (across == down)
    rank = jnp.sum(jnp.where(earlier, 1.0, 0.0), axis=1, keepdims=True)
    at_rank = rank == lane.astype(jnp.float32)
    for p in PARTS:
        listed = jnp.where(at_rank & (down == p), code, 0.0)
        entries = jnp.sum(listed, axis=0, keepdims=True).astype(jnp.int32) + SPARE
        size = jnp.sum(jnp.where(part == p, 1.0, 0.0), axis=1, keepdims=True)
        held[pl.ds(p, 1), :CAP] = entries
        held[pl.ds(p, 1), CAP:] = jnp.broadcast_to(size, (1, WIDTH - CAP)).astype(jnp.int32)
    copy = pltpu.make_async_copy(held, out, sems.at[2])
    copy.start()
    copy.wait()


def first_forward_kernel(
    count, row_ids, col_ids, tiles, x0, x1, out, buffer, lists, acc, rows, cols, held, sems, ids_sems
):
    chunks = (count[0] + CHUNK - 1) // CHUNK

    @pl.loop(0, chunks)
    def _(c):
        tile_copy(tiles, buffer, sems, c).start()

    make_lists(count, row_ids, col_ids, lists, rows, cols, held, ids_sems)
    acc[...] = jnp.zeros_like(acc)

    def ready(done, need):
        @pl.loop(done, need)
        def _(c):
            tile_copy(tiles, buffer, sems, c).wait()

        return jnp.maximum(done, need)

    works = ((OWN, forward_group(buffer, x0, acc)), (OWN_OTHER, forward_group(buffer, x1, acc)))
    counts = [lists[part, COUNT_AT] for part, _ in works]

    def step(k, done):
        base = k * CHUNK
        for (part, group), size in zip(works, counts):
            last = lists[part, jnp.maximum(jnp.minimum(base + CHUNK, size) - 1, 0)] & 255
            done = ready(done, jnp.where(base < size, last // CHUNK + 1, done))

            @pl.when(base < size)
            def _():
                group([lists[part, base + u] for u in range(CHUNK)])

        return done

    done = lax.fori_loop(0, (jnp.maximum(*counts) + CHUNK - 1) // CHUNK, step, 0)
    ready(done, chunks)
    out[...] = acc[:ROWS]


def forward_kernel(part, lists, buffer, before, x, out, acc):
    acc[:ROWS] = before[...]
    tile_groups(part, lists, forward_group(buffer, x, acc))
    out[...] = acc[:ROWS].astype(out.dtype)


def away_part_kernel(part, lists, buffer, got, out, acc, weight_sum):
    acc[...] = jnp.zeros_like(acc)
    nodes = got.shape[1] - BLOCK // 2
    weight_sum[...] = sum(got[k, nodes:].astype(jnp.float32) for k in range(got.shape[0]))
    tile_groups(part, lists, backward_group(buffer, got, acc))
    out[:SPAN] = acc[:PART].reshape(SPAN, out.shape[1]).astype(out.dtype)
    core = lax.axis_index("core")
    at = pl.multiple_of((core if part == BESIDE else 1 - core) * EXTRA, EXTRA)
    out[SPAN:] = weight_sum[pl.ds(at, EXTRA), :].astype(out.dtype)


def home_part_kernel(lists, buffer, got, own, other, acc, acc_other):
    for part, out, sums in ((OWN_OTHER, other, acc_other), (OWN, own, acc)):
        sums[...] = jnp.zeros_like(sums)
        tile_groups(part, lists, backward_group(buffer, got, sums))
        out[...] = sums[:PART].reshape(out.shape).astype(out.dtype)


def middle_kernel(y_parts, weight, cotangent, z_out, sent):
    reps, nodes, feats = y_parts.shape
    y = sum(y_parts[k].astype(jnp.float32) for k in range(reps))
    z = jnp.dot(
        y,
        weight[...].astype(jnp.float32),
        precision=lax.Precision.HIGHEST,
        preferred_element_type=jnp.float32,
    )
    sigma = jax.nn.sigmoid(z)
    z_out[...] = z
    grad = cotangent[...].astype(jnp.float32) * sigma * (1.0 + z * (1.0 - sigma))
    weight_part = jnp.dot(
        y.T.astype(jnp.bfloat16), grad.astype(jnp.bfloat16), preferred_element_type=jnp.float32
    ).astype(jnp.bfloat16)
    for at in range(0, nodes, BLOCK):
        grad_t = grad[at : at + BLOCK].T.astype(jnp.bfloat16)
        for k in range(reps):
            sent[k, pl.ds(at, BLOCK), :] = grad_t
    for k in range(reps):
        at = k % 2 * (BLOCK // 2)
        sent[k, nodes:] = weight_part[at : at + BLOCK // 2]


def hidden_kernel(z, hidden):
    hidden[...] = (z[...] * jax.nn.sigmoid(z[...])).astype(jnp.bfloat16)


def away_kernel(own, other, out):
    out[...] = (own[...] + other[...].astype(jnp.float32)).astype(jnp.bfloat16)


def home_kernel(own, other, away_own, away_other, came, out):
    peers = out.shape[0]
    nodes = out.shape[1] - EXTRA
    weight = away_own[SPAN:] + away_other[SPAN:].astype(jnp.float32)
    weight = (weight + came[SPAN:].astype(jnp.float32)).astype(jnp.bfloat16)
    for k in range(peers):
        here = pl.ds(k * nodes, nodes)
        total = own[here, :] + other[here, :].astype(jnp.float32)
        total = total + came[here, :].astype(jnp.float32)
        out[k, :nodes] = total.astype(jnp.bfloat16)
        out[k, nodes:] = weight


def weight_kernel(got, weight_rows):
    nodes = got.shape[1] - EXTRA
    weight_rows[...] = sum(got[k, nodes:].astype(jnp.float32) for k in range(got.shape[0]))


def feats_kernel(got, weight, grad_feats):
    nodes = grad_feats.shape[0]
    for at in range(0, nodes, BLOCK):
        here = pl.ds(at, BLOCK)
        total = sum(got[k, here].astype(jnp.float32) for k in range(got.shape[0]))
        grad_feats[here, :] = lax.dot_general(
            total.T.astype(jnp.bfloat16),
            weight[...],
            (((1,), (1,)), ((), ())),
            preferred_element_type=jnp.float32,
        ).astype(jnp.bfloat16)


def join_kernel(mine, over_core, over_ylo, over_both, grad_weight):
    core, ylo = lax.axis_index("core"), lax.axis_index("ylo")
    places = (
        (mine, ylo, core),
        (over_core, ylo, 1 - core),
        (over_ylo, 1 - ylo, core),
        (over_both, 1 - ylo, 1 - core),
    )
    for part, half, quarter in places:
        at = pl.multiple_of((half * 2 + quarter) * EXTRA, EXTRA)
        grad_weight[pl.ds(at, EXTRA), :] = part[...]


def fan_kernel(block, out, sem):
    copy = pltpu.make_async_copy(block, out.at[0], sem)
    copy.start()
    copy.wait()
    for k in range(1, out.shape[0]):
        out[k] = out[0]


SMEM = pl.BSMEM = pl.BSMEM = pl.BlockSpec(memory_space=pltpu.SMEM)
VMEM = pl.BlockSpec(memory_space=pltpu.VMEM)
ANY = pl.BlockSpec(memory_space=pl.ANY)


def tile_kernel(kernel, out_shape, lists, held, arrays, scratch):
    out_specs = (VMEM,) * len(out_shape) if isinstance(out_shape, tuple) else VMEM
    return pl.pallas_call(
        kernel,
        out_shape=out_shape,
        in_specs=[SMEM, VMEM] + [VMEM] * len(arrays),
        out_specs=out_specs,
        scratch_shapes=scratch,
        compiler_params=pltpu.CompilerParams(vmem_limit_bytes=16 << 20),
        cost_estimate=pl.CostEstimate(flops=1 << 29, bytes_accessed=4 << 20, transcendentals=0),
        name=getattr(kernel, "func", kernel).__name__,
    )(
        pltpu.with_memory_space_constraint(lists, pltpu.SMEM),
        pltpu.with_memory_space_constraint(held, pltpu.VMEM),
        *arrays,
    )


def sums(rows):
    return pltpu.VMEM((rows + 1, BLOCK, BLOCK), jnp.float32)


def merge(kernel, out_shape, *arrays):
    out_specs = (VMEM,) * len(out_shape) if isinstance(out_shape, tuple) else VMEM
    return pl.pallas_call(
        kernel,
        out_shape=out_shape,
        in_specs=[VMEM] * len(arrays),
        out_specs=out_specs,
        compiler_params=pltpu.CompilerParams(vmem_limit_bytes=16 << 20),
        cost_estimate=pl.CostEstimate(flops=1 << 20, bytes_accessed=4 << 20, transcendentals=0),
        name=kernel.__name__,
    )(*arrays)


def spread(block, axes):
    n = lax.axis_size(axes)
    blocks = pl.pallas_call(
        fan_kernel,
        out_shape=pltpu.VMEM((n, *block.shape), block.dtype),
        in_specs=[ANY],
        out_specs=VMEM,
        scratch_shapes=[pltpu.SemaphoreType.DMA],
        compiler_params=pltpu.CompilerParams(vmem_limit_bytes=16 << 20),
        cost_estimate=pl.CostEstimate(flops=0, bytes_accessed=1 << 16, transcendentals=0),
        name="fan",
    )(pltpu.with_memory_space_constraint(block, pltpu.HBM))
    return lax.all_to_all(blocks, axes, 0, 0)


def local(features, weight, cotangent, tiles, row_ids, col_ids, counts):
    x = features[0]
    nodes, feats = x.shape
    tiles = tiles[0, 0]
    blocks = (PART, BLOCK, feats)
    own = spread(x, PARITY)
    beside = lax.ppermute(own, ALONG, NEXT)
    own_other = lax.ppermute(own, "core", SWAP)
    y_shape = jax.ShapeDtypeStruct((ROWS, BLOCK, BLOCK), jnp.float32)
    y_part, held, lists = pl.pallas_call(
        first_forward_kernel,
        out_shape=(
            y_shape,
            pltpu.VMEM(tiles.shape, jnp.bfloat16),
            pltpu.SMEM((len(PARTS), WIDTH), jnp.int32),
        ),
        in_specs=[SMEM, ANY, ANY, ANY, VMEM, VMEM],
        out_specs=(VMEM, VMEM, SMEM),
        scratch_shapes=[
            sums(ROWS),
            pltpu.VMEM((1, CAP), jnp.int32),
            pltpu.VMEM((1, CAP), jnp.int32),
            pltpu.VMEM((len(PARTS), WIDTH), jnp.int32),
            pltpu.SemaphoreType.DMA((CAP // CHUNK,)),
            pltpu.SemaphoreType.DMA((3,)),
        ],
        compiler_params=pltpu.CompilerParams(vmem_limit_bytes=16 << 20),
        cost_estimate=pl.CostEstimate(flops=1 << 30, bytes_accessed=9 << 20, transcendentals=0),
        name="first_forward",
    )(
        counts[0],
        *[pltpu.with_memory_space_constraint(a, pltpu.HBM) for a in (row_ids[0], col_ids[0], tiles)],
        own.reshape(blocks),
        own_other.reshape(blocks),
    )
    beside, y_part = lax.optimization_barrier((beside, y_part))
    beside_other = lax.ppermute(beside, "core", SWAP)
    y_part = tile_kernel(
        functools.partial(forward_kernel, BESIDE),
        y_shape, lists, held, (y_part, beside.reshape(blocks)), [sums(ROWS)],
    )
    y_part = tile_kernel(
        functools.partial(forward_kernel, BESIDE_OTHER),
        jax.ShapeDtypeStruct((ROWS, BLOCK, BLOCK), jnp.bfloat16),
        lists, held, (y_part, beside_other.reshape(blocks)), [sums(ROWS)],
    )

    reps = lax.axis_size(REP)
    y_parts = lax.all_to_all(y_part.reshape(reps, nodes, feats), REP, 0, 0)
    z, sent = pl.pallas_call(
        middle_kernel,
        out_shape=(
            jax.ShapeDtypeStruct((nodes, feats), jnp.float32),
            pltpu.VMEM((reps, nodes + feats // 2, feats), jnp.bfloat16),
        ),
        in_specs=[VMEM, VMEM, VMEM],
        out_specs=(VMEM, VMEM),
        compiler_params=pltpu.CompilerParams(vmem_limit_bytes=16 << 20),
        cost_estimate=pl.CostEstimate(flops=1 << 25, bytes_accessed=4 << 20, transcendentals=1 << 15),
        name="middle",
    )(y_parts, weight, cotangent[0])
    got = lax.all_to_all(sent, REP, 0, 0)
    def away_part(part, dtype):
        return tile_kernel(
            functools.partial(away_part_kernel, part),
            jax.ShapeDtypeStruct((SPAN + EXTRA, feats), dtype),
            lists, held, (got,), [sums(PART), pltpu.VMEM((BLOCK // 2, feats), jnp.float32)],
        )

    away_other = lax.ppermute(away_part(BESIDE_OTHER, jnp.bfloat16), "core", SWAP)
    away_own = away_part(BESIDE, jnp.float32)
    away = merge(
        away_kernel, jax.ShapeDtypeStruct(away_own.shape, jnp.bfloat16), away_own, away_other
    )
    held, z, away = lax.optimization_barrier((held, z, away))
    came = lax.ppermute(away, ALONG, NEXT)
    home_own, home_other = tile_kernel(
        home_part_kernel,
        (
            jax.ShapeDtypeStruct((SPAN, feats), jnp.float32),
            jax.ShapeDtypeStruct((SPAN, feats), jnp.bfloat16),
        ),
        lists, held, (got,), [sums(PART), sums(PART)],
    )
    hidden = merge(hidden_kernel, jax.ShapeDtypeStruct((nodes, feats), jnp.bfloat16), z)
    home_other, hidden = lax.optimization_barrier((home_other, hidden))
    home_other = lax.ppermute(home_other, "core", SWAP)
    peers = lax.axis_size(PARITY)
    sent = merge(
        home_kernel,
        pltpu.VMEM((peers, nodes + EXTRA, feats), jnp.bfloat16),
        home_own, home_other, away_own, away_other, came,
    )
    got = lax.all_to_all(sent, PARITY, 0, 0)
    mine = merge(weight_kernel, jax.ShapeDtypeStruct((EXTRA, feats), jnp.float32), got)
    others = (
        lax.ppermute(mine, "ylo", SWAP),
        lax.ppermute(mine, ("ylo", "core"), ((0, 3), (1, 2), (2, 1), (3, 0))),
    )
    over_core = lax.ppermute(mine, "core", SWAP)
    grad_feats = merge(
        feats_kernel, jax.ShapeDtypeStruct((nodes, feats), jnp.bfloat16), got, weight
    )
    grad_weight = merge(
        join_kernel, jax.ShapeDtypeStruct((feats, feats), jnp.float32), mine, over_core, *others
    )
    return hidden[None], grad_feats.reshape(1, nodes, feats), grad_weight


def solution(mesh):
    mesh = Mesh(mesh.devices.reshape(SIZES), AXES)
    placed = P(ROW, REP)
    return jax.shard_map(
        local,
        mesh=mesh,
        in_specs=(placed, P(), placed, placed, placed, placed, placed),
        out_specs=(placed, placed, P()),
        check_vma=False,
    )
```

```python
import functools

import jax
import jax.numpy as jnp
from jax import lax
from jax.experimental import pallas as pl
from jax.experimental.pallas import tpu as pltpu
from jax.sharding import Mesh, PartitionSpec as P

CHUNK = 32
BLOCK = 128
ROWS = 16
PART = 16
CAP = 256
OWN, OWN_OTHER, BESIDE, BESIDE_OTHER = PARTS = range(4)
ROW_AT, PLACE_AT = 8, 13
SPARE = (ROWS << ROW_AT) | (PART << PLACE_AT)
COUNT_AT = CAP
WIDTH = CAP + 128
SPAN = PART * BLOCK
EXTRA = BLOCK // 4
SIZES = (4, 2, 2, 4, 2, 2)
AXES = ("x", "ylo", "yhi", "zq", "zp", "core")
REP = ("x", "ylo")
ROW = ("yhi", "zq", "zp", "core")
PARITY = ("yhi", "zq")
ALONG = ("zq", "zp", "core")
SWAP = ((0, 1), (1, 0))
NEXT = tuple((2 * z, 2 * ((z + 1) % 8)) for z in range(8)) + tuple(
    (2 * z + 1, 2 * ((z + 7) % 8) + 1) for z in range(8)
)


def tile_copy(tiles, buffer, sems, chunk):
    span = pl.ds(chunk * CHUNK, CHUNK)
    return pltpu.make_async_copy(tiles.at[span], buffer.at[span], sems.at[chunk])


def tile_groups(part, lists, group):
    @pl.loop(0, (lists[part, COUNT_AT] + CHUNK - 1) // CHUNK)
    def _(k):
        group([lists[part, k * CHUNK + u] for u in range(CHUNK)])


def forward_group(buffer, block_ref, acc):
    def group(codes):
        products = [
            jnp.dot(
                buffer[code & 255],
                block_ref[(code >> PLACE_AT) & (PART - 1)],
                preferred_element_type=jnp.float32,
            )
            for code in codes
        ]
        for code, product in zip(codes, products):
            acc[(code >> ROW_AT) & 31] += product

    return group


def backward_group(buffer, got, acc):
    def group(codes):
        products = []
        for code in codes:
            row = (code >> ROW_AT) & (ROWS - 1)
            grad = got[row // 2, pl.ds(pl.multiple_of((row % 2) * BLOCK, BLOCK), BLOCK), :]
            products.append(
                jnp.dot(grad, buffer[code & 255], preferred_element_type=jnp.float32)
            )
        for code, product in zip(codes, products):
            acc[code >> PLACE_AT] += product

    return group


def make_lists(count, row_ids, col_ids, out, rows, cols, held, sems):
    moves = [
        pltpu.make_async_copy(row_ids, rows, sems.at[0]),
        pltpu.make_async_copy(col_ids, cols, sems.at[1]),
    ]
    for move in moves:
        move.start()
    for move in moves:
        move.wait()
    slots = lax.broadcasted_iota(jnp.int32, (1, CAP), 1)
    block = cols[...]
    z = (block >> 2) & 7
    core = ((block >> 1) & 1) ^ lax.axis_index("core")
    part = ((z & 1) ^ lax.axis_index("zp")) * 2 + core
    place = ((block >> 5) * 4 + (z >> 1)) * 2 + (block & 1)
    code = slots | (rows[...] << ROW_AT) | (place << PLACE_AT)
    part = jnp.where(slots < count[0], part, len(PARTS)).astype(jnp.float32)
    code = (code - SPARE).astype(jnp.float32)

    square = (CAP, CAP)
    across = jnp.broadcast_to(part, square)
    down = across.T
    code = jnp.broadcast_to(code, square).T
    lane = lax.broadcasted_iota(jnp.int32, square, 1)
    earlier = (lane < lax.broadcasted_iota(jnp.int32, square, 0)) & (across == down)
    rank = jnp.sum(jnp.where(earlier, 1.0, 0.0), axis=1, keepdims=True)
    at_rank = rank == lane.astype(jnp.float32)
    for p in PARTS:
        listed = jnp.where(at_rank & (down == p), code, 0.0)
        entries = jnp.sum(listed, axis=0, keepdims=True).astype(jnp.int32) + SPARE
        size = jnp.sum(jnp.where(part == p, 1.0, 0.0), axis=1, keepdims=True)
        held[pl.ds(p, 1), :CAP] = entries
        held[pl.ds(p, 1), CAP:] = jnp.broadcast_to(size, (1, WIDTH - CAP)).astype(jnp.int32)
    copy = pltpu.make_async_copy(held, out, sems.at[2])
    copy.start()
    copy.wait()


def first_forward_kernel(
    count, row_ids, col_ids, tiles, x0, x1, out, buffer, lists, acc, rows, cols, held, sems, ids_sems
):
    chunks = (count[0] + CHUNK - 1) // CHUNK

    @pl.loop(0, chunks)
    def _(c):
        tile_copy(tiles, buffer, sems, c).start()

    make_lists(count, row_ids, col_ids, lists, rows, cols, held, ids_sems)
    acc[...] = jnp.zeros_like(acc)

    def ready(done, need):
        @pl.loop(done, need)
        def _(c):
            tile_copy(tiles, buffer, sems, c).wait()

        return jnp.maximum(done, need)

    works = ((OWN, forward_group(buffer, x0, acc)), (OWN_OTHER, forward_group(buffer, x1, acc)))
    counts = [lists[part, COUNT_AT] for part, _ in works]

    def step(k, done):
        base = k * CHUNK
        for (part, group), size in zip(works, counts):
            last = lists[part, jnp.maximum(jnp.minimum(base + CHUNK, size) - 1, 0)] & 255
            done = ready(done, jnp.where(base < size, last // CHUNK + 1, done))

            @pl.when(base < size)
            def _():
                group([lists[part, base + u] for u in range(CHUNK)])

        return done

    done = lax.fori_loop(0, (jnp.maximum(*counts) + CHUNK - 1) // CHUNK, step, 0)
    ready(done, chunks)
    out[...] = acc[:ROWS]


def forward_kernel(part, lists, buffer, before, x, out, acc):
    acc[:ROWS] = before[...]
    tile_groups(part, lists, forward_group(buffer, x, acc))
    out[...] = acc[:ROWS].astype(out.dtype)


def away_part_kernel(part, lists, buffer, got, out, acc):
    acc[...] = jnp.zeros_like(acc)
    nodes = got.shape[1] - BLOCK // 2
    tile_groups(part, lists, backward_group(buffer, got, acc))
    out[:SPAN] = acc[:PART].reshape(SPAN, out.shape[1]).astype(out.dtype)
    core = lax.axis_index("core")
    at = nodes + pl.multiple_of((core if part == BESIDE else 1 - core) * EXTRA, EXTRA)
    rows = pl.ds(pl.multiple_of(at, EXTRA), EXTRA)
    total = sum(got[k, rows, :].astype(jnp.float32) for k in range(got.shape[0]))
    out[SPAN:] = total.astype(out.dtype)


def home_part_kernel(lists, buffer, got, own, other, acc, acc_other):
    for part, out, sums in ((OWN_OTHER, other, acc_other), (OWN, own, acc)):
        sums[...] = jnp.zeros_like(sums)
        tile_groups(part, lists, backward_group(buffer, got, sums))
        out[...] = sums[:PART].reshape(out.shape).astype(out.dtype)


def middle_kernel(y_parts, weight, cotangent, z_out, sent):
    reps, nodes, feats = y_parts.shape
    y = sum(y_parts[k].astype(jnp.float32) for k in range(reps))
    high = y.astype(jnp.bfloat16)
    low = (y - high.astype(jnp.float32)).astype(jnp.bfloat16)
    z = jnp.dot(high, weight[...], preferred_element_type=jnp.float32)
    z = z + jnp.dot(low, weight[...], preferred_element_type=jnp.float32)
    sigma = jax.nn.sigmoid(z)
    z_out[...] = z
    grad = cotangent[...].astype(jnp.float32) * sigma * (1.0 + z * (1.0 - sigma))
    weight_part = jnp.dot(
        y.T.astype(jnp.bfloat16), grad.astype(jnp.bfloat16), preferred_element_type=jnp.float32
    ).astype(jnp.bfloat16)
    for at in range(0, nodes, BLOCK):
        grad_t = grad[at : at + BLOCK].T.astype(jnp.bfloat16)
        for k in range(reps):
            sent[k, pl.ds(at, BLOCK), :] = grad_t
    for k in range(reps):
        at = k % 2 * (BLOCK // 2)
        sent[k, nodes:] = weight_part[at : at + BLOCK // 2]


def hidden_kernel(z, hidden):
    hidden[...] = (z[...] * jax.nn.sigmoid(z[...])).astype(jnp.bfloat16)


def away_kernel(own, other, out):
    out[...] = (own[...] + other[...].astype(jnp.float32)).astype(jnp.bfloat16)


def home_kernel(own, other, away_own, away_other, came, out):
    peers = out.shape[0]
    nodes = out.shape[1] - EXTRA
    weight = away_own[SPAN:] + away_other[SPAN:].astype(jnp.float32)
    weight = (weight + came[SPAN:].astype(jnp.float32)).astype(jnp.bfloat16)
    for k in range(peers):
        here = pl.ds(k * nodes, nodes)
        total = own[here, :] + other[here, :].astype(jnp.float32)
        total = total + came[here, :].astype(jnp.float32)
        out[k, :nodes] = total.astype(jnp.bfloat16)
        out[k, nodes:] = weight


def weight_kernel(got, weight_rows):
    nodes = got.shape[1] - EXTRA
    weight_rows[...] = sum(got[k, nodes:].astype(jnp.float32) for k in range(got.shape[0]))


def feats_kernel(got, weight, grad_feats):
    nodes = grad_feats.shape[0]
    for at in range(0, nodes, BLOCK):
        here = pl.ds(at, BLOCK)
        total = sum(got[k, here].astype(jnp.float32) for k in range(got.shape[0]))
        grad_feats[here, :] = lax.dot_general(
            total.T.astype(jnp.bfloat16),
            weight[...],
            (((1,), (1,)), ((), ())),
            preferred_element_type=jnp.float32,
        ).astype(jnp.bfloat16)


def join_kernel(mine, over_core, over_ylo, over_both, grad_weight):
    core, ylo = lax.axis_index("core"), lax.axis_index("ylo")
    places = (
        (mine, ylo, core),
        (over_core, ylo, 1 - core),
        (over_ylo, 1 - ylo, core),
        (over_both, 1 - ylo, 1 - core),
    )
    for part, half, quarter in places:
        at = pl.multiple_of((half * 2 + quarter) * EXTRA, EXTRA)
        grad_weight[pl.ds(at, EXTRA), :] = part[...]


def fan_kernel(block, out, sem):
    copy = pltpu.make_async_copy(block, out.at[0], sem)
    copy.start()
    copy.wait()
    for k in range(1, out.shape[0]):
        out[k] = out[0]


SMEM = pl.BSMEM = pl.BSMEM = pl.BlockSpec(memory_space=pltpu.SMEM)
VMEM = pl.BlockSpec(memory_space=pltpu.VMEM)
ANY = pl.BlockSpec(memory_space=pl.ANY)


def tile_kernel(kernel, out_shape, lists, held, arrays, scratch):
    out_specs = (VMEM,) * len(out_shape) if isinstance(out_shape, tuple) else VMEM
    return pl.pallas_call(
        kernel,
        out_shape=out_shape,
        in_specs=[SMEM, VMEM] + [VMEM] * len(arrays),
        out_specs=out_specs,
        scratch_shapes=scratch,
        compiler_params=pltpu.CompilerParams(vmem_limit_bytes=16 << 20),
        cost_estimate=pl.CostEstimate(flops=1 << 29, bytes_accessed=4 << 20, transcendentals=0),
        name=getattr(kernel, "func", kernel).__name__,
    )(
        pltpu.with_memory_space_constraint(lists, pltpu.SMEM),
        pltpu.with_memory_space_constraint(held, pltpu.VMEM),
        *arrays,
    )


def sums(rows):
    return pltpu.VMEM((rows + 1, BLOCK, BLOCK), jnp.float32)


def merge(kernel, out_shape, *arrays):
    out_specs = (VMEM,) * len(out_shape) if isinstance(out_shape, tuple) else VMEM
    return pl.pallas_call(
        kernel,
        out_shape=out_shape,
        in_specs=[VMEM] * len(arrays),
        out_specs=out_specs,
        compiler_params=pltpu.CompilerParams(vmem_limit_bytes=16 << 20),
        cost_estimate=pl.CostEstimate(flops=1 << 20, bytes_accessed=4 << 20, transcendentals=0),
        name=kernel.__name__,
    )(*arrays)


def spread(block, axes):
    n = lax.axis_size(axes)
    blocks = pl.pallas_call(
        fan_kernel,
        out_shape=pltpu.VMEM((n, *block.shape), block.dtype),
        in_specs=[ANY],
        out_specs=VMEM,
        scratch_shapes=[pltpu.SemaphoreType.DMA],
        compiler_params=pltpu.CompilerParams(vmem_limit_bytes=16 << 20),
        cost_estimate=pl.CostEstimate(flops=0, bytes_accessed=1 << 16, transcendentals=0),
        name="fan",
    )(pltpu.with_memory_space_constraint(block, pltpu.HBM))
    return lax.all_to_all(blocks, axes, 0, 0)


def local(features, weight, cotangent, tiles, row_ids, col_ids, counts):
    x = features[0]
    nodes, feats = x.shape
    tiles = tiles[0, 0]
    blocks = (PART, BLOCK, feats)
    own = spread(x, PARITY)
    beside = lax.ppermute(own, ALONG, NEXT)
    own_other = lax.ppermute(own, "core", SWAP)
    y_shape = jax.ShapeDtypeStruct((ROWS, BLOCK, BLOCK), jnp.float32)
    y_part, held, lists = pl.pallas_call(
        first_forward_kernel,
        out_shape=(
            y_shape,
            pltpu.VMEM(tiles.shape, jnp.bfloat16),
            pltpu.SMEM((len(PARTS), WIDTH), jnp.int32),
        ),
        in_specs=[SMEM, ANY, ANY, ANY, VMEM, VMEM],
        out_specs=(VMEM, VMEM, SMEM),
        scratch_shapes=[
            sums(ROWS),
            pltpu.VMEM((1, CAP), jnp.int32),
            pltpu.VMEM((1, CAP), jnp.int32),
            pltpu.VMEM((len(PARTS), WIDTH), jnp.int32),
            pltpu.SemaphoreType.DMA((CAP // CHUNK,)),
            pltpu.SemaphoreType.DMA((3,)),
        ],
        compiler_params=pltpu.CompilerParams(vmem_limit_bytes=16 << 20),
        cost_estimate=pl.CostEstimate(flops=1 << 30, bytes_accessed=9 << 20, transcendentals=0),
        name="first_forward",
    )(
        counts[0],
        *[pltpu.with_memory_space_constraint(a, pltpu.HBM) for a in (row_ids[0], col_ids[0], tiles)],
        own.reshape(blocks),
        own_other.reshape(blocks),
    )
    beside, y_part = lax.optimization_barrier((beside, y_part))
    beside_other = lax.ppermute(beside, "core", SWAP)
    y_part = tile_kernel(
        functools.partial(forward_kernel, BESIDE),
        y_shape, lists, held, (y_part, beside.reshape(blocks)), [sums(ROWS)],
    )
    y_part = tile_kernel(
        functools.partial(forward_kernel, BESIDE_OTHER),
        jax.ShapeDtypeStruct((ROWS, BLOCK, BLOCK), jnp.bfloat16),
        lists, held, (y_part, beside_other.reshape(blocks)), [sums(ROWS)],
    )

    reps = lax.axis_size(REP)
    y_parts = lax.all_to_all(y_part.reshape(reps, nodes, feats), REP, 0, 0)
    z, sent = pl.pallas_call(
        middle_kernel,
        out_shape=(
            jax.ShapeDtypeStruct((nodes, feats), jnp.float32),
            pltpu.VMEM((reps, nodes + feats // 2, feats), jnp.bfloat16),
        ),
        in_specs=[VMEM, VMEM, VMEM],
        out_specs=(VMEM, VMEM),
        compiler_params=pltpu.CompilerParams(vmem_limit_bytes=16 << 20),
        cost_estimate=pl.CostEstimate(flops=1 << 25, bytes_accessed=4 << 20, transcendentals=1 << 15),
        name="middle",
    )(y_parts, weight, cotangent[0])
    got = lax.all_to_all(sent, REP, 0, 0)
    def away_part(part, dtype):
        return tile_kernel(
            functools.partial(away_part_kernel, part),
            jax.ShapeDtypeStruct((SPAN + EXTRA, feats), dtype),
            lists, held, (got,), [sums(PART)],
        )

    away_other = lax.ppermute(away_part(BESIDE_OTHER, jnp.bfloat16), "core", SWAP)
    away_own = away_part(BESIDE, jnp.float32)
    away = merge(
        away_kernel, jax.ShapeDtypeStruct(away_own.shape, jnp.bfloat16), away_own, away_other
    )
    held, z, away = lax.optimization_barrier((held, z, away))
    came = lax.ppermute(away, ALONG, NEXT)
    home_own, home_other = tile_kernel(
        home_part_kernel,
        (
            jax.ShapeDtypeStruct((SPAN, feats), jnp.float32),
            jax.ShapeDtypeStruct((SPAN, feats), jnp.bfloat16),
        ),
        lists, held, (got,), [sums(PART), sums(PART)],
    )
    hidden = merge(hidden_kernel, jax.ShapeDtypeStruct((nodes, feats), jnp.bfloat16), z)
    home_other, hidden = lax.optimization_barrier((home_other, hidden))
    home_other = lax.ppermute(home_other, "core", SWAP)
    peers = lax.axis_size(PARITY)
    sent = merge(
        home_kernel,
        pltpu.VMEM((peers, nodes + EXTRA, feats), jnp.bfloat16),
        home_own, home_other, away_own, away_other, came,
    )
    got = lax.all_to_all(sent, PARITY, 0, 0)
    mine = merge(weight_kernel, jax.ShapeDtypeStruct((EXTRA, feats), jnp.float32), got)
    others = (
        lax.ppermute(mine, "ylo", SWAP),
        lax.ppermute(mine, ("ylo", "core"), ((0, 3), (1, 2), (2, 1), (3, 0))),
    )
    over_core = lax.ppermute(mine, "core", SWAP)
    grad_feats = merge(
        feats_kernel, jax.ShapeDtypeStruct((nodes, feats), jnp.bfloat16), got, weight
    )
    grad_weight = merge(
        join_kernel, jax.ShapeDtypeStruct((feats, feats), jnp.float32), mine, over_core, *others
    )
    return hidden[None], grad_feats.reshape(1, nodes, feats), grad_weight


def solution(mesh):
    mesh = Mesh(mesh.devices.reshape(SIZES), AXES)
    placed = P(ROW, REP)
    return jax.shard_map(
        local,
        mesh=mesh,
        in_specs=(placed, P(), placed, placed, placed, placed, placed),
        out_specs=(placed, placed, P()),
        check_vma=False,
    )
```

```python
import functools

import jax
import jax.numpy as jnp
from jax import lax
from jax.experimental import pallas as pl
from jax.experimental.pallas import tpu as pltpu
from jax.sharding import Mesh, PartitionSpec as P

CHUNK = 32
BLOCK = 128
ROWS = 16
PART = 16
CAP = 256
OWN, OWN_OTHER, BESIDE, BESIDE_OTHER = PARTS = range(4)
ROW_AT, PLACE_AT = 8, 13
SPARE = (ROWS << ROW_AT) | (PART << PLACE_AT)
COUNT_AT = CAP
WIDTH = CAP + 128
SPAN = PART * BLOCK
EXTRA = BLOCK // 4
SIZES = (4, 2, 2, 4, 2, 2)
AXES = ("x", "ylo", "yhi", "zq", "zp", "core")
REP = ("x", "ylo")
ROW = ("yhi", "zq", "zp", "core")
PARITY = ("yhi", "zq")
ALONG = ("zq", "zp", "core")
SWAP = ((0, 1), (1, 0))
NEXT = tuple((2 * z, 2 * ((z + 1) % 8)) for z in range(8)) + tuple(
    (2 * z + 1, 2 * ((z + 7) % 8) + 1) for z in range(8)
)


def tile_copy(tiles, buffer, sems, chunk):
    span = pl.ds(chunk * CHUNK, CHUNK)
    return pltpu.make_async_copy(tiles.at[span], buffer.at[span], sems.at[chunk])


def tile_groups(part, lists, group):
    @pl.loop(0, (lists[part, COUNT_AT] + CHUNK - 1) // CHUNK)
    def _(k):
        group([lists[part, k * CHUNK + u] for u in range(CHUNK)])


def forward_group(buffer, block_ref, acc):
    def group(codes):
        products = [
            jnp.dot(
                buffer[code & 255],
                block_ref[(code >> PLACE_AT) & (PART - 1)],
                preferred_element_type=jnp.float32,
            )
            for code in codes
        ]
        for code, product in zip(codes, products):
            acc[(code >> ROW_AT) & 31] += product

    return group


def backward_group(buffer, got, acc):
    def group(codes):
        products = []
        for code in codes:
            row = (code >> ROW_AT) & (ROWS - 1)
            grad = got[row // 2, pl.ds(pl.multiple_of((row % 2) * BLOCK, BLOCK), BLOCK), :]
            products.append(
                jnp.dot(grad, buffer[code & 255], preferred_element_type=jnp.float32)
            )
        for code, product in zip(codes, products):
            acc[code >> PLACE_AT] += product

    return group


def make_lists(count, row_ids, col_ids, out, rows, cols, held, sems):
    moves = [
        pltpu.make_async_copy(row_ids, rows, sems.at[0]),
        pltpu.make_async_copy(col_ids, cols, sems.at[1]),
    ]
    for move in moves:
        move.start()
    for move in moves:
        move.wait()
    slots = lax.broadcasted_iota(jnp.int32, (1, CAP), 1)
    block = cols[...]
    z = (block >> 2) & 7
    core = ((block >> 1) & 1) ^ lax.axis_index("core")
    part = ((z & 1) ^ lax.axis_index("zp")) * 2 + core
    place = ((block >> 5) * 4 + (z >> 1)) * 2 + (block & 1)
    code = slots | (rows[...] << ROW_AT) | (place << PLACE_AT)
    part = jnp.where(slots < count[0], part, len(PARTS)).astype(jnp.float32)
    code = (code - SPARE).astype(jnp.float32)

    square = (CAP, CAP)
    across = jnp.broadcast_to(part, square)
    down = across.T
    code = jnp.broadcast_to(code, square).T
    lane = lax.broadcasted_iota(jnp.int32, square, 1)
    earlier = (lane < lax.broadcasted_iota(jnp.int32, square, 0)) & (across == down)
    rank = jnp.sum(jnp.where(earlier, 1.0, 0.0), axis=1, keepdims=True)
    at_rank = rank == lane.astype(jnp.float32)
    for p in PARTS:
        listed = jnp.where(at_rank & (down == p), code, 0.0)
        entries = jnp.sum(listed, axis=0, keepdims=True).astype(jnp.int32) + SPARE
        size = jnp.sum(jnp.where(part == p, 1.0, 0.0), axis=1, keepdims=True)
        held[pl.ds(p, 1), :CAP] = entries
        held[pl.ds(p, 1), CAP:] = jnp.broadcast_to(size, (1, WIDTH - CAP)).astype(jnp.int32)
    copy = pltpu.make_async_copy(held, out, sems.at[2])
    copy.start()
    copy.wait()


def first_forward_kernel(
    count, row_ids, col_ids, tiles, x0, x1, out, buffer, lists, acc, rows, cols, held, sems, ids_sems
):
    chunks = (count[0] + CHUNK - 1) // CHUNK

    @pl.loop(0, chunks)
    def _(c):
        tile_copy(tiles, buffer, sems, c).start()

    make_lists(count, row_ids, col_ids, lists, rows, cols, held, ids_sems)
    acc[...] = jnp.zeros_like(acc)

    def ready(done, need):
        @pl.loop(done, need)
        def _(c):
            tile_copy(tiles, buffer, sems, c).wait()

        return jnp.maximum(done, need)

    works = ((OWN, forward_group(buffer, x0, acc)), (OWN_OTHER, forward_group(buffer, x1, acc)))
    counts = [lists[part, COUNT_AT] for part, _ in works]

    def step(k, done):
        base = k * CHUNK
        for (part, group), size in zip(works, counts):
            last = lists[part, jnp.maximum(jnp.minimum(base + CHUNK, size) - 1, 0)] & 255
            done = ready(done, jnp.where(base < size, last // CHUNK + 1, done))

            @pl.when(base < size)
            def _():
                group([lists[part, base + u] for u in range(CHUNK)])

        return done

    done = lax.fori_loop(0, (jnp.maximum(*counts) + CHUNK - 1) // CHUNK, step, 0)
    ready(done, chunks)
    out[...] = acc[:ROWS]


def forward_kernel(part, lists, buffer, before, x, out, acc):
    acc[:ROWS] = before[...]
    tile_groups(part, lists, forward_group(buffer, x, acc))
    out[...] = acc[:ROWS].astype(out.dtype)


def away_part_kernel(part, lists, buffer, got, out, acc):
    acc[...] = jnp.zeros_like(acc)
    nodes = got.shape[1] - BLOCK // 2
    tile_groups(part, lists, backward_group(buffer, got, acc))
    out[:SPAN] = acc[:PART].reshape(SPAN, out.shape[1]).astype(out.dtype)
    core = lax.axis_index("core")
    at = nodes + pl.multiple_of((core if part == BESIDE else 1 - core) * EXTRA, EXTRA)
    rows = pl.ds(pl.multiple_of(at, EXTRA), EXTRA)
    total = sum(got[k, rows, :].astype(jnp.float32) for k in range(got.shape[0]))
    out[SPAN:] = total.astype(out.dtype)


def home_part_kernel(lists, buffer, got, own, other, acc, acc_other):
    for part, out, sums in ((OWN_OTHER, other, acc_other), (OWN, own, acc)):
        sums[...] = jnp.zeros_like(sums)
        tile_groups(part, lists, backward_group(buffer, got, sums))
        out[...] = sums[:PART].reshape(out.shape).astype(out.dtype)


def middle_kernel(y_parts, weight, cotangent, z_out, sent):
    reps, nodes, feats = y_parts.shape
    y = sum(y_parts[k].astype(jnp.float32) for k in range(reps))
    high = y.astype(jnp.bfloat16)
    low = (y - high.astype(jnp.float32)).astype(jnp.bfloat16)
    z = jnp.dot(high, weight[...], preferred_element_type=jnp.float32)
    z = z + jnp.dot(low, weight[...], preferred_element_type=jnp.float32)
    sigma = jax.nn.sigmoid(z)
    z_out[...] = z
    grad = cotangent[...].astype(jnp.float32) * sigma * (1.0 + z * (1.0 - sigma))
    weight_part = jnp.dot(
        high.T, grad.astype(jnp.bfloat16), preferred_element_type=jnp.float32
    ).astype(jnp.bfloat16)
    for at in range(0, nodes, BLOCK):
        grad_t = grad[at : at + BLOCK].T.astype(jnp.bfloat16)
        for k in range(reps):
            sent[k, pl.ds(at, BLOCK), :] = grad_t
    for k in range(reps):
        at = k % 2 * (BLOCK // 2)
        sent[k, nodes:] = weight_part[at : at + BLOCK // 2]


def hidden_kernel(z, hidden):
    hidden[...] = (z[...] * jax.nn.sigmoid(z[...])).astype(jnp.bfloat16)


def away_kernel(own, other, out):
    out[...] = (own[...] + other[...].astype(jnp.float32)).astype(jnp.bfloat16)


def home_kernel(own, other, away_own, away_other, came, out):
    peers = out.shape[0]
    nodes = out.shape[1] - EXTRA
    weight = away_own[SPAN:] + away_other[SPAN:].astype(jnp.float32)
    weight = (weight + came[SPAN:].astype(jnp.float32)).astype(jnp.bfloat16)
    for k in range(peers):
        here = pl.ds(k * nodes, nodes)
        total = own[here, :] + other[here, :].astype(jnp.float32)
        total = total + came[here, :].astype(jnp.float32)
        out[k, :nodes] = total.astype(jnp.bfloat16)
        out[k, nodes:] = weight


def weight_kernel(got, weight_rows):
    nodes = got.shape[1] - EXTRA
    weight_rows[...] = sum(got[k, nodes:].astype(jnp.float32) for k in range(got.shape[0]))


def feats_kernel(got, weight, grad_feats):
    nodes = grad_feats.shape[0]
    for at in range(0, nodes, BLOCK):
        here = pl.ds(at, BLOCK)
        total = sum(got[k, here].astype(jnp.float32) for k in range(got.shape[0]))
        grad_feats[here, :] = lax.dot_general(
            total.T.astype(jnp.bfloat16),
            weight[...],
            (((1,), (1,)), ((), ())),
            preferred_element_type=jnp.float32,
        ).astype(jnp.bfloat16)


def join_kernel(mine, over_core, over_ylo, over_both, grad_weight):
    core, ylo = lax.axis_index("core"), lax.axis_index("ylo")
    places = (
        (mine, ylo, core),
        (over_core, ylo, 1 - core),
        (over_ylo, 1 - ylo, core),
        (over_both, 1 - ylo, 1 - core),
    )
    for part, half, quarter in places:
        at = pl.multiple_of((half * 2 + quarter) * EXTRA, EXTRA)
        grad_weight[pl.ds(at, EXTRA), :] = part[...]


def fan_kernel(block, out, sem):
    copy = pltpu.make_async_copy(block, out.at[0], sem)
    copy.start()
    copy.wait()
    for k in range(1, out.shape[0]):
        out[k] = out[0]


SMEM = pl.BSMEM = pl.BSMEM = pl.BlockSpec(memory_space=pltpu.SMEM)
VMEM = pl.BlockSpec(memory_space=pltpu.VMEM)
ANY = pl.BlockSpec(memory_space=pl.ANY)


def tile_kernel(kernel, out_shape, lists, held, arrays, scratch):
    out_specs = (VMEM,) * len(out_shape) if isinstance(out_shape, tuple) else VMEM
    return pl.pallas_call(
        kernel,
        out_shape=out_shape,
        in_specs=[SMEM, VMEM] + [VMEM] * len(arrays),
        out_specs=out_specs,
        scratch_shapes=scratch,
        compiler_params=pltpu.CompilerParams(vmem_limit_bytes=16 << 20),
        cost_estimate=pl.CostEstimate(flops=1 << 29, bytes_accessed=4 << 20, transcendentals=0),
        name=getattr(kernel, "func", kernel).__name__,
    )(
        pltpu.with_memory_space_constraint(lists, pltpu.SMEM),
        pltpu.with_memory_space_constraint(held, pltpu.VMEM),
        *arrays,
    )


def sums(rows):
    return pltpu.VMEM((rows + 1, BLOCK, BLOCK), jnp.float32)


def merge(kernel, out_shape, *arrays):
    out_specs = (VMEM,) * len(out_shape) if isinstance(out_shape, tuple) else VMEM
    return pl.pallas_call(
        kernel,
        out_shape=out_shape,
        in_specs=[VMEM] * len(arrays),
        out_specs=out_specs,
        compiler_params=pltpu.CompilerParams(vmem_limit_bytes=16 << 20),
        cost_estimate=pl.CostEstimate(flops=1 << 20, bytes_accessed=4 << 20, transcendentals=0),
        name=kernel.__name__,
    )(*arrays)


def spread(block, axes):
    n = lax.axis_size(axes)
    blocks = pl.pallas_call(
        fan_kernel,
        out_shape=pltpu.VMEM((n, *block.shape), block.dtype),
        in_specs=[ANY],
        out_specs=VMEM,
        scratch_shapes=[pltpu.SemaphoreType.DMA],
        compiler_params=pltpu.CompilerParams(vmem_limit_bytes=16 << 20),
        cost_estimate=pl.CostEstimate(flops=0, bytes_accessed=1 << 16, transcendentals=0),
        name="fan",
    )(pltpu.with_memory_space_constraint(block, pltpu.HBM))
    return lax.all_to_all(blocks, axes, 0, 0)


def local(features, weight, cotangent, tiles, row_ids, col_ids, counts):
    x = features[0]
    nodes, feats = x.shape
    tiles = tiles[0, 0]
    blocks = (PART, BLOCK, feats)
    own = spread(x, PARITY)
    beside = lax.ppermute(own, ALONG, NEXT)
    own_other = lax.ppermute(own, "core", SWAP)
    y_shape = jax.ShapeDtypeStruct((ROWS, BLOCK, BLOCK), jnp.float32)
    y_part, held, lists = pl.pallas_call(
        first_forward_kernel,
        out_shape=(
            y_shape,
            pltpu.VMEM(tiles.shape, jnp.bfloat16),
            pltpu.SMEM((len(PARTS), WIDTH), jnp.int32),
        ),
        in_specs=[SMEM, ANY, ANY, ANY, VMEM, VMEM],
        out_specs=(VMEM, VMEM, SMEM),
        scratch_shapes=[
            sums(ROWS),
            pltpu.VMEM((1, CAP), jnp.int32),
            pltpu.VMEM((1, CAP), jnp.int32),
            pltpu.VMEM((len(PARTS), WIDTH), jnp.int32),
            pltpu.SemaphoreType.DMA((CAP // CHUNK,)),
            pltpu.SemaphoreType.DMA((3,)),
        ],
        compiler_params=pltpu.CompilerParams(vmem_limit_bytes=16 << 20),
        cost_estimate=pl.CostEstimate(flops=1 << 30, bytes_accessed=9 << 20, transcendentals=0),
        name="first_forward",
    )(
        counts[0],
        *[pltpu.with_memory_space_constraint(a, pltpu.HBM) for a in (row_ids[0], col_ids[0], tiles)],
        own.reshape(blocks),
        own_other.reshape(blocks),
    )
    beside, y_part = lax.optimization_barrier((beside, y_part))
    beside_other = lax.ppermute(beside, "core", SWAP)
    y_part = tile_kernel(
        functools.partial(forward_kernel, BESIDE),
        y_shape, lists, held, (y_part, beside.reshape(blocks)), [sums(ROWS)],
    )
    y_part = tile_kernel(
        functools.partial(forward_kernel, BESIDE_OTHER),
        jax.ShapeDtypeStruct((ROWS, BLOCK, BLOCK), jnp.bfloat16),
        lists, held, (y_part, beside_other.reshape(blocks)), [sums(ROWS)],
    )

    reps = lax.axis_size(REP)
    y_parts = lax.all_to_all(y_part.reshape(reps, nodes, feats), REP, 0, 0)
    z, sent = pl.pallas_call(
        middle_kernel,
        out_shape=(
            jax.ShapeDtypeStruct((nodes, feats), jnp.float32),
            pltpu.VMEM((reps, nodes + feats // 2, feats), jnp.bfloat16),
        ),
        in_specs=[VMEM, VMEM, VMEM],
        out_specs=(VMEM, VMEM),
        compiler_params=pltpu.CompilerParams(vmem_limit_bytes=16 << 20),
        cost_estimate=pl.CostEstimate(flops=1 << 25, bytes_accessed=4 << 20, transcendentals=1 << 15),
        name="middle",
    )(y_parts, weight, cotangent[0])
    got = lax.all_to_all(sent, REP, 0, 0)
    def away_part(part, dtype):
        return tile_kernel(
            functools.partial(away_part_kernel, part),
            jax.ShapeDtypeStruct((SPAN + EXTRA, feats), dtype),
            lists, held, (got,), [sums(PART)],
        )

    away_other = lax.ppermute(away_part(BESIDE_OTHER, jnp.bfloat16), "core", SWAP)
    away_own = away_part(BESIDE, jnp.float32)
    away = merge(
        away_kernel, jax.ShapeDtypeStruct(away_own.shape, jnp.bfloat16), away_own, away_other
    )
    held, z, away = lax.optimization_barrier((held, z, away))
    came = lax.ppermute(away, ALONG, NEXT)
    home_own, home_other = tile_kernel(
        home_part_kernel,
        (
            jax.ShapeDtypeStruct((SPAN, feats), jnp.float32),
            jax.ShapeDtypeStruct((SPAN, feats), jnp.bfloat16),
        ),
        lists, held, (got,), [sums(PART), sums(PART)],
    )
    hidden = merge(hidden_kernel, jax.ShapeDtypeStruct((nodes, feats), jnp.bfloat16), z)
    home_other, hidden = lax.optimization_barrier((home_other, hidden))
    home_other = lax.ppermute(home_other, "core", SWAP)
    peers = lax.axis_size(PARITY)
    sent = merge(
        home_kernel,
        pltpu.VMEM((peers, nodes + EXTRA, feats), jnp.bfloat16),
        home_own, home_other, away_own, away_other, came,
    )
    got = lax.all_to_all(sent, PARITY, 0, 0)
    mine = merge(weight_kernel, jax.ShapeDtypeStruct((EXTRA, feats), jnp.float32), got)
    others = (
        lax.ppermute(mine, "ylo", SWAP),
        lax.ppermute(mine, ("ylo", "core"), ((0, 3), (1, 2), (2, 1), (3, 0))),
    )
    over_core = lax.ppermute(mine, "core", SWAP)
    grad_feats = merge(
        feats_kernel, jax.ShapeDtypeStruct((nodes, feats), jnp.bfloat16), got, weight
    )
    grad_weight = merge(
        join_kernel, jax.ShapeDtypeStruct((feats, feats), jnp.float32), mine, over_core, *others
    )
    return hidden[None], grad_feats.reshape(1, nodes, feats), grad_weight


def solution(mesh):
    mesh = Mesh(mesh.devices.reshape(SIZES), AXES)
    placed = P(ROW, REP)
    return jax.shard_map(
        local,
        mesh=mesh,
        in_specs=(placed, P(), placed, placed, placed, placed, placed),
        out_specs=(placed, placed, P()),
        check_vma=False,
    )
```
